32 devices in a mesh: tex: 16 (over z, x, core), view: 2 (over y).
Axes of the slice: x: 2, y: 2, z: 4, core: 2. Of those that a mesh axis runs over, the one named last changes fastest.
Arguments:
- measured: bfloat16 [384, 160, 151], P('tex', 'view'), may hold values from -6 to 6
- view_mask: int32 [160], P('view'), may hold values from 0 to 1, as said below
- tex_factor: float32 [384, 256], P('tex'), may hold values from -6 to 6
- view_factor: float32 [160, 64], P('view'), as said below
- light_factor: bfloat16 [151, 64], replicated, as said below
- core_tensor: float32 [256, 64, 64], P('tex', 'view'), may hold values from -6 to 6
Outputs:
- tex_updated: float32 [384, 256], P('tex')
- view_updated: float32 [160, 64], P('view')
- core_updated: float32 [256, 64, 64], P('tex', 'view')
The draws below stay inside these ranges and needn't reach their ends.
Inputs may be any that keep to these rules, and one draw needn't show every extreme that they name: `view_mask`: exactly 151 of the 160 entries are 1. `view_factor`: entries of order one. `light_factor`: entries of order one.
All inputs are finite; a program needn't handle non-finite values.
Results may differ from the reference program's by a relative error of at most 0.014.
Values may be sent and summed in bfloat16 or wider, within the bound.
A program may use at most 64 MiB of HBM per device.

```python
import math
import jax
import jax.numpy as jnp
from jax import lax

RT = 256
RV = 64
RL = 64
VIEWS = 160
VALID = 151
L = 151
TD = 24
STEPS = 1
TEXELS = 384
N_VIEW = 2


def spread_columns(key, rows, cols):
    sample = jax.random.normal(key, (rows, cols), jnp.float32)
    matrix = sample / jnp.linalg.norm(sample)
    for sweep in range(30):
        gram_matrix = jnp.dot(matrix.T, matrix, precision=lax.Precision.HIGHEST)
        matrix = 1.5 * matrix - 0.5 * jnp.dot(matrix, gram_matrix, precision=lax.Precision.HIGHEST)
    return matrix * math.sqrt(rows)


def draw_view_mask(key, part):
    order = jax.random.permutation(jax.random.fold_in(key, 11), VIEWS)
    return (order < VALID).astype(jnp.int32)


def draw_view_factor(key, part):
    return spread_columns(jax.random.fold_in(key, 23), VIEWS, RV)


def draw_light_factor(key, part):
    return spread_columns(jax.random.fold_in(key, 37), L, RL).astype(jnp.bfloat16)


def shard_levels(own_key, shape, pieces, smallest, high):
    loudness, own = 1.0, jax.random.fold_in(own_key, 6)
    for position, shards_of in pieces:
        heights = jnp.exp(jax.random.uniform(jax.random.fold_in(own, position), (shards_of,), jnp.float32, smallest / len(pieces), high / len(pieces)))
        loudness = loudness * jnp.repeat(heights, shape[position] // shards_of).reshape([-1 if axis == position else 1 for axis in range(len(shape))])
    return loudness


def noise(stream_key, shape, scale, bound, split=(), held_as=jnp.bfloat16):
    factor_of = shard_levels(stream_key, shape, split, -0.22, 0.18) if split else 1.0
    values = jax.random.normal(stream_key, shape, jnp.float32) * scale * factor_of
    return jnp.minimum(jnp.maximum(values, -bound), bound).astype(held_as)


def setup_inputs(seed: int = 0) -> dict:
    arg_keys = jax.random.split(jax.random.key(seed), 7)
    return {
        "measured": noise(arg_keys[0], (TEXELS, VIEWS, L), 1.0, 6.0, ((0, 16), (1, 2))),
        "view_mask": draw_view_mask(jax.random.fold_in(arg_keys[6], 71), 0),
        "tex_factor": noise(arg_keys[2], (TEXELS, RT), 1.0, 6.0, ((0, 16),), jnp.float32),
        "view_factor": draw_view_factor(jax.random.fold_in(arg_keys[6], 71), 0),
        "light_factor": draw_light_factor(jax.random.fold_in(arg_keys[6], 71), 0),
        "core_tensor": noise(arg_keys[5], (RT, RV, RL), 1.0, 6.0, ((0, 16), (1, 2)), jnp.float32),
    }


def round_trip(values):
    return lax.optimization_barrier(values.astype(jnp.bfloat16)).astype(jnp.float32)

def reference(measured, view_mask, tex_factor, view_factor, light_factor, core_tensor):
    scaling = (RT * RV * RL) ** (-0.5)
    rate_tex = RT / (VALID * L)
    rate_view = RV / (TEXELS * L)
    rate_core = RT * RV * RL / (TEXELS * VALID * L)
    weights = view_mask.astype(jnp.float32)[None, :, None]
    light_full = light_factor.astype(jnp.float32)
    blocks = measured.reshape(TEXELS // TD, TD, VIEWS, L)
    tex_now = tex_factor
    view_now = view_factor
    core_now = core_tensor
    for iteration in range(STEPS):
        tex_bf = tex_now.astype(jnp.bfloat16)
        view_bf = view_now.astype(jnp.bfloat16)
        core_bf = core_now.astype(jnp.bfloat16)
        core_flat = core_bf.reshape(RT, RV * RL)
        projected = jnp.dot(tex_bf.astype(jnp.float32), core_flat.astype(jnp.float32), preferred_element_type=jnp.float32).astype(jnp.bfloat16)
        proj_blocks = projected.reshape(TEXELS // TD, TD, RV, RL)
        view_full = view_bf.astype(jnp.float32)
        view_groups = view_full.reshape(N_VIEW, VIEWS // N_VIEW, RV)

        def per_block(total, inputs):
            sample, proj_block = inputs
            proj_full = proj_block.astype(jnp.float32)
            mixed = round_trip(jnp.einsum('vb,tbc->tvc', view_full, proj_full))
            approx = jnp.einsum('tvc,lc->tvl', mixed, light_full)
            resid = round_trip(weights * (scaling * approx - sample.astype(jnp.float32)))
            back = round_trip(jnp.einsum('tvl,lc->tvc', resid, light_full))
            grad_part = scaling * jnp.einsum('tvc,tbc->vb', back, proj_full)
            grouped = back.reshape(TD, N_VIEW, VIEWS // N_VIEW, RL)
            partials = round_trip(jnp.einsum('gvb,tgvc->tgbc', view_groups, grouped))
            return (total + grad_part, jnp.sum(partials, axis=1).astype(jnp.bfloat16))
        grad_view, summed = lax.scan(per_block, jnp.zeros((VIEWS, RV), jnp.float32), (blocks, proj_blocks))
        summed_flat = summed.reshape(TEXELS, RV * RL)
        grad_tex = scaling * lax.dot_general(summed_flat.astype(jnp.float32), core_flat.astype(jnp.float32), (((1,), (1,)), ((), ())), preferred_element_type=jnp.float32)
        grad_core = scaling * lax.dot_general(tex_bf.astype(jnp.float32), summed_flat.astype(jnp.float32), (((0,), (0,)), ((), ())), preferred_element_type=jnp.float32)
        tex_now = tex_now - rate_tex * grad_tex
        view_now = view_now - rate_view * grad_view
        core_now = core_now - rate_core * grad_core.reshape(RT, RV, RL)
    return (tex_now, view_now, core_now)
```

```python
import functools

import jax
import jax.numpy as jnp
from jax import lax
from jax.experimental import pallas as pl
from jax.experimental.pallas import tpu as pltpu
from jax.sharding import PartitionSpec as P

RT = 256
RV = 64
RL = 64
VALID = 151
L = 151
LINE = 4
GROUP = 256 // RL
LIGHTS = 256 * (-(-L // 256))
SCALING = (RT * RV * RL) ** (-0.5)
MESH = pl.DeviceIdType.MESH
BF = jnp.bfloat16
F32 = jnp.float32
NT = (((1,), (1,)), ((), ()))
TN = (((0,), (0,)), ((), ()))


def kernel(
    tex_count, view_count,
    g_ref, u_ref, v_ref, mask_ref, light_ref, meas_hbm,
    gu_ref, gv_ref, gg_ref,
    gbuf, meas, bdw, rbuf, p3, pall, ysend, yrecv, ysum, yflat,
    us, ur, gvs, gvr, rs, rc, xr, zr,
    meas_sem, ga_s, gb_s, gc_s, g_r, p_s, p_r, y_s, y_r, u_s, u_r, gv_s, gv_r,
    c_s, c_r, x_s, x_r, z_s, z_r,
):
    na = LINE
    nb = tex_count // (2 * na)
    me = lax.axis_index("tex")
    view = lax.axis_index("view")
    core = lax.rem(me, 2)
    b = lax.rem(me // 2, nb)
    a = me // (2 * nb)
    rows, width = g_ref.shape
    band = width // RL
    texels = u_ref.shape[0]
    groups = texels // GROUP
    steps = tex_count.bit_length() - 1

    def slot(ai, bi, ci):
        return (ai * nb + bi) * 2 + ci

    def push(src, dst, ssem, rsem, tex, vw):
        copy = pltpu.make_async_remote_copy(
            src_ref=src, dst_ref=dst, send_sem=ssem, recv_sem=rsem,
            device_id=(tex, vw), device_id_type=MESH,
        )
        copy.start()
        return copy

    def arrived(ref, sem):
        pltpu.make_async_copy(ref, ref, sem).wait()

    sibling = slot(a, b, 1 - core)
    pending = []

    for d in range(1, na):
        pending.append(push(g_ref, gbuf.at[me], ga_s.at[d - 1], g_r.at[me],
                            slot(lax.rem(a + d, na), b, core), view))
    for e in range(1, nb):
        pending.append(push(g_ref, gbuf.at[me], gb_s.at[0, e - 1], g_r.at[me],
                            slot(a, lax.rem(b + e, nb), core), view))
    pending.append(push(g_ref, gbuf.at[me], gc_s.at[0, 0], g_r.at[me], sibling, view))
    meas_copy = pltpu.make_async_copy(meas_hbm, meas, meas_sem)
    meas_copy.start()
    gbuf[me] = g_ref[...]

    bdw[...] = jnp.zeros_like(bdw)
    rbuf[...] = jnp.zeros_like(rbuf)
    for j in range(GROUP):
        bdw[j * LIGHTS:j * LIGHTS + L, j * RL:(j + 1) * RL] = light_ref[...]

    def across(d):
        ad = lax.rem(a + na - d, na)
        for e in range(1, nb):
            s = slot(ad, lax.rem(b + nb - e, nb), core)
            arrived(gbuf.at[s], g_r.at[s])
            pending.append(push(gbuf.at[s], gbuf.at[s], gc_s.at[d, e], g_r.at[s], sibling, view))

    for d in range(1, na):
        s = slot(lax.rem(a + na - d, na), b, core)
        arrived(gbuf.at[s], g_r.at[s])
        for e in range(1, nb):
            pending.append(push(gbuf.at[s], gbuf.at[s], gb_s.at[d, e - 1], g_r.at[s],
                                slot(a, lax.rem(b + e, nb), core), view))
        pending.append(push(gbuf.at[s], gbuf.at[s], gc_s.at[d, 0], g_r.at[s], sibling, view))
        across(d - 1)
    across(na - 1)
    for ai in range(na):
        for bi in range(nb):
            s = slot(ai, bi, 1 - core)
            arrived(gbuf.at[s], g_r.at[s])

    u_bf = u_ref[...].astype(BF)
    v_bf = v_ref[...].astype(BF)
    if rows % 16 == 0:
        g_all = gbuf[...].reshape(tex_count * rows, width)
    else:
        g_all = jnp.concatenate(
            [gbuf[j].astype(F32) for j in range(tex_count)], axis=0).astype(BF)

    proj = jnp.dot(u_bf, g_all, preferred_element_type=F32)
    for j in range(band):
        p3[j] = proj[:, j * RL:(j + 1) * RL]
    for t in range(0, texels, 2):
        pair = jnp.concatenate([p3[:, t, :], p3[:, t + 1, :]], axis=1)
        pall[view, :, t * RL:(t + 2) * RL] = pair.astype(BF)
    for w in range(1, view_count):
        pending.append(push(pall.at[view], pall.at[view], p_s.at[w - 1], p_r.at[view],
                            me, lax.rem(view + w, view_count)))
    meas_copy.wait()
    weights = mask_ref[...].astype(F32)
    for w in range(1, view_count):
        other = lax.rem(view + w, view_count)
        arrived(pall.at[other], p_r.at[other])

    gv = jnp.zeros(gv_ref.shape, F32)
    for k in range(groups):
        lanes = slice(k * GROUP * RL, (k + 1) * GROUP * RL)
        if band % 16 == 0:
            p4 = jnp.concatenate([pall[w, :, lanes] for w in range(view_count)], axis=0)
        else:
            p4 = jnp.concatenate(
                [pall[w, :, lanes].astype(F32) for w in range(view_count)], axis=0).astype(BF)
        q4 = jnp.dot(v_bf, p4, preferred_element_type=F32).astype(BF)
        a4 = lax.dot_general(q4, bdw[...], NT, preferred_element_type=F32)
        for j in range(GROUP):
            part = a4[:, j * LIGHTS:j * LIGHTS + L]
            resid = weights * (SCALING * part - meas[k * GROUP + j].astype(F32))
            rbuf[k, :, j * LIGHTS:j * LIGHTS + L] = resid.astype(BF)
        s4 = jnp.dot(rbuf[k], bdw[...], preferred_element_type=F32).astype(BF)
        gv = gv + lax.dot_general(s4, p4, NT, preferred_element_type=F32)
        y4 = lax.dot_general(v_bf, s4, TN, preferred_element_type=F32)
        for w in range(view_count):
            ysend[w, :, lanes] = y4[w * band:(w + 1) * band].astype(BF)

    for w in range(1, view_count):
        other = lax.rem(view + w, view_count)
        pending.append(push(ysend.at[other], yrecv.at[w - 1], y_s.at[w - 1], y_r.at[w - 1],
                            me, other))

    def gv_start(i, value):
        gvs[i] = value
        partner = me + (1 << i) - 2 * (1 << i) * lax.rem(me // (1 << i), 2)
        pending.append(push(gvs.at[i], gvr.at[i], gv_s.at[i], gv_r.at[i], partner, view))

    def gv_next(i):
        arrived(gvr.at[i], gv_r.at[i])
        value = gvs[i] + gvr[i]
        if i + 1 < steps:
            gv_start(i + 1, value)
        else:
            gv_ref[...] = value

    gv_start(0, SCALING * gv)

    for w in range(1, view_count):
        arrived(yrecv.at[w - 1], y_r.at[w - 1])
    total = ysend[view].astype(F32)
    for w in range(1, view_count):
        total = total + yrecv[w - 1].astype(F32)
    for t in range(texels):
        ysum[:, t, :] = total[:, t * RL:(t + 1) * RL]
    for j in range(0, band, 2):
        pair = jnp.concatenate([ysum[j], ysum[j + 1]], axis=1)
        yflat[:, j * RL:(j + 2) * RL] = pair.astype(BF)
    gv_next(0)

    y_bf = yflat[...]
    grad = SCALING * lax.dot_general(u_bf, y_bf, TN, preferred_element_type=F32)
    for j in range(tex_count):
        rs[j] = grad[j * rows:(j + 1) * rows].astype(BF)

    order = [d % na for d in range(1, na + 1)]
    for e in list(range(1, nb)) + [0]:
        for d in order:
            ad, be = lax.rem(a + d, na), lax.rem(b + e, nb)
            pending.append(push(rs.at[slot(ad, be, 1 - core)], rc.at[d, e], c_s.at[d, e], c_r.at[d, e],
                                sibling, view))

    us[...] = SCALING * lax.dot_general(y_bf, g_all, NT, preferred_element_type=F32)
    for w in range(1, view_count):
        pending.append(push(us, ur.at[w - 1], u_s.at[w - 1], u_r.at[w - 1],
                            me, lax.rem(view + w, view_count)))
    if steps > 1:
        gv_next(1)

    for e in range(1, nb):
        for d in order:
            ad, be = lax.rem(a + d, na), lax.rem(b + e, nb)
            s = slot(ad, be, core)
            arrived(rc.at[d, e], c_r.at[d, e])
            rs[s] = (rs[s].astype(F32) + rc[d, e].astype(F32)).astype(BF)
            pending.append(push(rs.at[s], xr.at[d, e - 1], x_s.at[d, e - 1], x_r.at[d, e - 1],
                                slot(a, be, core), view))
    if steps > 2:
        gv_next(2)
    for d in order:
        s = slot(lax.rem(a + d, na), b, core)
        arrived(rc.at[d, 0], c_r.at[d, 0])
        block = rs[s].astype(F32) + rc[d, 0].astype(F32)
        for e in range(1, nb):
            arrived(xr.at[d, e - 1], x_r.at[d, e - 1])
            block = block + xr[d, e - 1].astype(F32)
        if d:
            rs[s] = block.astype(BF)
            pending.append(push(rs.at[s], zr.at[d - 1], z_s.at[d - 1], z_r.at[d - 1],
                                slot(lax.rem(a + d, na), b, core), view))
    for i in range(3, steps):
        gv_next(i)

    total_u = us[...]
    for w in range(1, view_count):
        arrived(ur.at[w - 1], u_r.at[w - 1])
        total_u = total_u + ur[w - 1]
    gu_ref[...] = total_u
    for d in range(1, na):
        arrived(zr.at[d - 1], z_r.at[d - 1])
        block = block + zr[d - 1].astype(F32)
    gg_ref[...] = block
    for copy in pending:
        copy.wait_send()


def per_device(measured, view_mask, tex_factor, view_factor, light_factor, core_tensor):
    tex_count = lax.axis_size("tex")
    view_count = lax.axis_size("view")
    texels, views, _ = measured.shape
    rows, band, _ = core_tensor.shape
    width = band * RL
    texels_all = texels * tex_count
    nb = tex_count // (2 * LINE)
    steps = tex_count.bit_length() - 1
    peers = max(view_count - 1, 1)
    rate_tex = RT / (VALID * L)
    rate_view = RV / (texels_all * L)
    rate_core = RT * RV * RL / (texels_all * VALID * L)
    vmem = pl.BlockSpec(memory_space=pltpu.VMEM)
    dma = pltpu.SemaphoreType.DMA
    gu, gv, gg = pl.pallas_call(
        functools.partial(kernel, tex_count, view_count),
        out_shape=(
            jax.ShapeDtypeStruct((texels, RT), F32),
            jax.ShapeDtypeStruct((views, RV), F32),
            jax.ShapeDtypeStruct((rows, width), F32),
        ),
        in_specs=[vmem] * 5 + [pl.BlockSpec(memory_space=pl.ANY)],
        out_specs=(vmem, vmem, vmem),
        scratch_shapes=[
            pltpu.VMEM((tex_count, rows, width), BF),
            pltpu.VMEM((texels, views, L), BF),
            pltpu.VMEM((GROUP * LIGHTS, GROUP * RL), BF),
            pltpu.VMEM((texels // GROUP, views, GROUP * LIGHTS), BF),
            pltpu.VMEM((band, texels, RL), F32),
            pltpu.VMEM((view_count, band, texels * RL), BF),
            pltpu.VMEM((view_count, band, texels * RL), BF),
            pltpu.VMEM((peers, band, texels * RL), BF),
            pltpu.VMEM((band, texels, RL), F32),
            pltpu.VMEM((texels, width), BF),
            pltpu.VMEM((texels, RT), F32),
            pltpu.VMEM((peers, texels, RT), F32),
            pltpu.VMEM((steps, views, RV), F32),
            pltpu.VMEM((steps, views, RV), F32),
            pltpu.VMEM((tex_count, rows, width), BF),
            pltpu.VMEM((LINE, nb, rows, width), BF),
            pltpu.VMEM((LINE, max(nb - 1, 1), rows, width), BF),
            pltpu.VMEM((LINE - 1, rows, width), BF),
            dma, dma((LINE - 1,)), dma((LINE, max(nb - 1, 1))), dma((LINE, nb)), dma((tex_count,)),
            dma((peers,)), dma((view_count,)), dma((peers,)), dma((peers,)),
            dma((peers,)), dma((peers,)), dma((steps,)), dma((steps,)),
            dma((LINE, nb)), dma((LINE, nb)),
            dma((LINE, max(nb - 1, 1))), dma((LINE, max(nb - 1, 1))),
            dma((LINE - 1,)), dma((LINE - 1,)),
        ],
        compiler_params=pltpu.CompilerParams(
            has_side_effects=True, vmem_limit_bytes=48 * 1024 * 1024),
        cost_estimate=pl.CostEstimate(flops=10**9, bytes_accessed=10**7, transcendentals=0),
    )(core_tensor.astype(BF).reshape(rows, width), tex_factor, view_factor,
      view_mask.reshape(views, 1), light_factor, measured)
    return (
        tex_factor - rate_tex * gu,
        view_factor - rate_view * gv,
        core_tensor - rate_core * gg.reshape(core_tensor.shape),
    )


def solution(mesh):
    return jax.shard_map(
        per_device,
        mesh=mesh,
        in_specs=(
            P("tex", "view", None),
            P("view"),
            P("tex", None),
            P("view", None),
            P(),
            P("tex", "view", None),
        ),
        out_specs=(P("tex", None), P("view", None), P("tex", "view", None)),
        check_vma=False,
    )
```

```python
import functools

import jax
import jax.numpy as jnp
from jax import lax
from jax.experimental import pallas as pl
from jax.experimental.pallas import tpu as pltpu
from jax.sharding import PartitionSpec as P

RT = 256
RV = 64
RL = 64
VALID = 151
L = 151
LINE = 4
CHUNKS = 2
GROUP = 256 // RL
LIGHTS = 256 * (-(-L // 256))
SCALING = (RT * RV * RL) ** (-0.5)
MESH = pl.DeviceIdType.MESH
BF = jnp.bfloat16
F32 = jnp.float32
NT = (((1,), (1,)), ((), ()))
TN = (((0,), (0,)), ((), ()))


def kernel(
    tex_count, view_count, rates,
    core_ref, u_ref, vt_ref, mask_ref, lightt_ref, meas_hbm,
    u_out, vt_out, core_out,
    gl, gbuf, meas, mwide, mturn, weights, vcol, vrow, bdw, qbuf, rbuf, p3, pall,
    ysend, yrecv, ysum, yflat, us, ur, gvs, gvr, rs, rc, xr, zr,
    meas_sem, ga_s, gb_s, gc_s, g_r, p_s, p_r, y_s, y_r, u_s, u_r, gv_s, gv_r,
    c_s, c_r, x_s, x_r, z_s, z_r,
):
    na = LINE
    nb = tex_count // (2 * na)
    me = lax.axis_index("tex")
    view = lax.axis_index("view")
    core = lax.rem(me, 2)
    b = lax.rem(me // 2, nb)
    a = me // (2 * nb)
    rows, band, _ = core_ref.shape
    part = band // CHUNKS
    texels = u_ref.shape[0]
    views = vt_ref.shape[1]
    padded = vcol.shape[0]
    groups = texels // GROUP
    steps = tex_count.bit_length() - 1
    rate_tex, rate_view, rate_core = rates

    def slot(ai, bi, ci):
        return (ai * nb + bi) * 2 + ci

    def ahead(d):
        return lax.rem(a + d, na)

    def beside(e):
        return lax.rem(b + e, nb)

    def other(w):
        return lax.rem(view + w, view_count)

    sibling = slot(a, b, 1 - core)
    pending = []

    def push(src, dst, ssem, rsem, tex, vw):
        copy = pltpu.make_async_remote_copy(
            src_ref=src, dst_ref=dst, send_sem=ssem, recv_sem=rsem,
            device_id=(tex, vw), device_id_type=MESH,
        )
        copy.start()
        pending.append(copy)

    def arrived(ref, sem):
        pltpu.make_async_copy(ref, ref, sem).wait()

    barrier = pltpu.get_barrier_semaphore()
    peers = [(slot(ahead(d), b, core), view) for d in range(1, na)]
    peers += [(slot(a, beside(e), core), view) for e in range(1, nb)]
    peers += [(sibling, view)]
    peers += [(me, other(w)) for w in range(1, view_count)]
    for peer in peers:
        pl.semaphore_signal(barrier, inc=1, device_id=peer, device_id_type=MESH)
    meas_copy = pltpu.make_async_copy(meas_hbm, meas, meas_sem)
    meas_copy.start()
    for i in range(0, band, 2):
        pair = jnp.concatenate([core_ref[:, i, :], core_ref[:, i + 1, :]], axis=1).astype(BF)
        h, o = divmod(i, part)
        gl[h, :, o * RL:(o + 2) * RL] = pair
    pl.semaphore_wait(barrier, len(peers))

    for h in range(CHUNKS):
        for e in range(1, nb):
            push(gl.at[h], gbuf.at[h, me], gb_s.at[h, 0, e - 1], g_r.at[h, me],
                 slot(a, beside(e), core), view)
        for d in range(1, na):
            push(gl.at[h], gbuf.at[h, me], ga_s.at[h, d - 1], g_r.at[h, me],
                 slot(ahead(d), b, core), view)
        push(gl.at[h], gbuf.at[h, me], gc_s.at[h, 0, 0], g_r.at[h, me], sibling, view)

    def from_line(h, d):
        s = slot(ahead(na - d), b, core)
        arrived(gbuf.at[h, s], g_r.at[h, s])
        for e in range(1, nb):
            push(gbuf.at[h, s], gbuf.at[h, s], gb_s.at[h, d, e - 1], g_r.at[h, s],
                 slot(a, beside(e), core), view)
        push(gbuf.at[h, s], gbuf.at[h, s], gc_s.at[h, d, 0], g_r.at[h, s], sibling, view)

    def from_across(h):
        for d in range(na):
            for e in range(1, nb):
                s = slot(ahead(na - d), beside(nb - e), core)
                arrived(gbuf.at[h, s], g_r.at[h, s])
                push(gbuf.at[h, s], gbuf.at[h, s], gc_s.at[h, d, e], g_r.at[h, s], sibling, view)

    for h in range(CHUNKS):
        gbuf[h, me] = gl[h]
    bdw[...] = jnp.zeros_like(bdw)
    rbuf[...] = jnp.zeros_like(rbuf)
    for j in range(GROUP):
        bdw[j * RL:(j + 1) * RL, j * LIGHTS:j * LIGHTS + L] = lightt_ref[...]
    vcol[...] = jnp.zeros_like(vcol)
    vrow[...] = jnp.zeros_like(vrow)
    vcol[:views, :] = vt_ref[...].T
    vrow[:, :views] = vt_ref[...]
    weights[...] = jnp.broadcast_to(mask_ref[...].astype(F32), (LIGHTS, views)).T
    meas_copy.wait()
    mwide[...] = meas[...].astype(F32)
    turns = -(-texels // (CHUNKS * (na - 1)))
    t = 0
    for h in range(CHUNKS):
        for d in range(1, na):
            from_line(h, d)
            for _ in range(turns):
                if t < texels:
                    mturn[t] = mwide[:, t, :].T
                    t += 1

    u_bf = u_ref[...].astype(BF)

    def stacked(h):
        if rows % 16 == 0:
            return gbuf[h].reshape(tex_count * rows, part * RL)
        return jnp.concatenate(
            [gbuf[h, j].astype(F32) for j in range(tex_count)], axis=0).astype(BF)

    for h in range(CHUNKS):
        from_across(h)
        for ai in range(na):
            for bi in range(nb):
                s = slot(ai, bi, 1 - core)
                arrived(gbuf.at[h, s], g_r.at[h, s])
        proj = jnp.dot(u_bf, stacked(h), preferred_element_type=F32)
        for j in range(part):
            p3[h, j] = proj[:, j * RL:(j + 1) * RL]
        for t in range(0, texels, 2):
            pair = jnp.concatenate([p3[h, :, t, :], p3[h, :, t + 1, :]], axis=1)
            pall[h, view, :, t * RL:(t + 2) * RL] = pair.astype(BF)
        for w in range(1, view_count):
            push(pall.at[h, view], pall.at[h, view], p_s.at[h, w - 1], p_r.at[h, view],
                 me, other(w))
    v_bf = vcol[...].astype(BF)
    vt_bf = vrow[...].astype(BF)
    for h in range(CHUNKS):
        for w in range(1, view_count):
            arrived(pall.at[h, other(w)], p_r.at[h, other(w)])

    def lanes(k):
        return slice(k * GROUP * RL, (k + 1) * GROUP * RL)

    def p_group(k):
        pieces = [pall[h, w, :, lanes(k)] for w in range(view_count) for h in range(CHUNKS)]
        if part % 16 == 0:
            return jnp.concatenate(pieces, axis=0)
        return jnp.concatenate([piece.astype(F32) for piece in pieces], axis=0).astype(BF)

    for k in range(groups):
        qbuf[k] = jnp.dot(v_bf, p_group(k), preferred_element_type=F32).astype(BF)
    q_all = qbuf[...].reshape(groups * padded, GROUP * RL)
    mask = weights[:, :L]
    for j in range(GROUP):
        cols = slice(j * LIGHTS, (j + 1) * LIGHTS)
        approx = jnp.dot(q_all, bdw[:, cols], preferred_element_type=F32)
        for k in range(groups):
            piece = approx[k * padded:k * padded + views, :L]
            resid = mask * (SCALING * piece - mturn[k * GROUP + j])
            rbuf[k, :views, j * LIGHTS:j * LIGHTS + L] = resid.astype(BF)
    r_all = rbuf[...].reshape(groups * padded, GROUP * LIGHTS)
    s_all = lax.dot_general(r_all, bdw[...], NT, preferred_element_type=F32).astype(BF)
    for k in range(groups):
        s4 = s_all[k * padded:(k + 1) * padded]
        y4 = jnp.dot(vt_bf, s4, preferred_element_type=F32).astype(BF)
        for w in range(view_count):
            for h in range(CHUNKS):
                first = w * band + h * part
                ysend[h, w, :, lanes(k)] = y4[first:first + part]
    for h in range(CHUNKS):
        for w in range(1, view_count):
            push(ysend.at[h, other(w)], yrecv.at[h, w - 1], y_s.at[h, w - 1], y_r.at[h, w - 1],
                 me, other(w))
    gv = jnp.zeros((RV, padded), F32)
    for k in range(groups):
        s4 = s_all[k * padded:(k + 1) * padded]
        gv = gv + lax.dot_general(p_group(k), s4, NT, preferred_element_type=F32)

    def gv_start(i, value):
        gvs[i] = value
        partner = me + (1 << i) - 2 * (1 << i) * lax.rem(me // (1 << i), 2)
        push(gvs.at[i], gvr.at[i], gv_s.at[i], gv_r.at[i], partner, view)

    def gv_next(i):
        arrived(gvr.at[i], gv_r.at[i])
        value = gvs[i] + gvr[i]
        if i + 1 < steps:
            gv_start(i + 1, value)
        else:
            vt_out[...] = vt_ref[...] - rate_view * value[:, :views]

    gv_start(0, SCALING * gv)

    order = [d % na for d in range(1, na + 1)]
    y_bf = []
    for h in range(CHUNKS):
        total = ysend[h, view].astype(F32)
        for w in range(1, view_count):
            arrived(yrecv.at[h, w - 1], y_r.at[h, w - 1])
            total = total + yrecv[h, w - 1].astype(F32)
        for t in range(texels):
            ysum[h, :, t, :] = total[:, t * RL:(t + 1) * RL]
        for j in range(0, part, 2):
            pair = jnp.concatenate([ysum[h, j], ysum[h, j + 1]], axis=1)
            yflat[h, :, j * RL:(j + 2) * RL] = pair.astype(BF)
        y_bf.append(yflat[h])
        grad = SCALING * lax.dot_general(u_bf, y_bf[h], TN, preferred_element_type=F32)
        for j in range(tex_count):
            rs[h, j] = grad[j * rows:(j + 1) * rows].astype(BF)
        for e in list(range(1, nb)) + [0]:
            for d in order:
                push(rs.at[h, slot(ahead(d), beside(e), 1 - core)], rc.at[h, d, e],
                     c_s.at[h, d, e], c_r.at[h, d, e], sibling, view)

    partial = jnp.zeros((texels, RT), F32)
    for h in range(CHUNKS):
        partial = partial + lax.dot_general(y_bf[h], stacked(h), NT, preferred_element_type=F32)
    us[...] = SCALING * partial
    for w in range(1, view_count):
        push(us, ur.at[w - 1], u_s.at[w - 1], u_r.at[w - 1], me, other(w))
    gv_next(0)

    for h in range(CHUNKS):
        for e in range(1, nb):
            for d in order:
                s = slot(ahead(d), beside(e), core)
                arrived(rc.at[h, d, e], c_r.at[h, d, e])
                rs[h, s] = (rs[h, s].astype(F32) + rc[h, d, e].astype(F32)).astype(BF)
                push(rs.at[h, s], xr.at[h, d, e - 1], x_s.at[h, d, e - 1], x_r.at[h, d, e - 1],
                     slot(a, beside(e), core), view)
        if h + 1 < steps:
            gv_next(h + 1)
    own = []
    for h in range(CHUNKS):
        for d in order:
            s = slot(ahead(d), b, core)
            arrived(rc.at[h, d, 0], c_r.at[h, d, 0])
            block = rs[h, s].astype(F32) + rc[h, d, 0].astype(F32)
            for e in range(1, nb):
                arrived(xr.at[h, d, e - 1], x_r.at[h, d, e - 1])
                block = block + xr[h, d, e - 1].astype(F32)
            if d:
                rs[h, s] = block.astype(BF)
                push(rs.at[h, s], zr.at[h, d - 1], z_s.at[h, d - 1], z_r.at[h, d - 1],
                     slot(ahead(d), b, core), view)
        own.append(block)
    for i in range(CHUNKS + 1, steps):
        gv_next(i)
    total_u = us[...]
    for w in range(1, view_count):
        arrived(ur.at[w - 1], u_r.at[w - 1])
        total_u = total_u + ur[w - 1]
    u_out[...] = u_ref[...] - rate_tex * total_u
    for h in range(CHUNKS):
        block = own[h]
        for d in range(1, na):
            arrived(zr.at[h, d - 1], z_r.at[h, d - 1])
            block = block + zr[h, d - 1].astype(F32)
        block = rate_core * block
        for j in range(part):
            i = h * part + j
            core_out[:, i, :] = core_ref[:, i, :] - block[:, j * RL:(j + 1) * RL]
    for copy in pending:
        copy.wait_send()


def per_device(measured, view_mask, tex_factor, view_factor, light_factor, core_tensor):
    tex_count = lax.axis_size("tex")
    view_count = lax.axis_size("view")
    texels, views, _ = measured.shape
    rows, band, _ = core_tensor.shape
    part = band // CHUNKS
    cut = part * RL
    texels_all = texels * tex_count
    nb = tex_count // (2 * LINE)
    steps = tex_count.bit_length() - 1
    peers = max(view_count - 1, 1)
    across = max(nb - 1, 1)
    padded = 16 * (-(-views // 16))
    groups = texels // GROUP
    rates = (
        RT / (VALID * L),
        RV / (texels_all * L),
        RT * RV * RL / (texels_all * VALID * L),
    )
    vmem = pl.BlockSpec(memory_space=pltpu.VMEM)
    dma = pltpu.SemaphoreType.DMA
    tex_new, view_new, core_new = pl.pallas_call(
        functools.partial(kernel, tex_count, view_count, rates),
        out_shape=(
            jax.ShapeDtypeStruct((texels, RT), F32),
            jax.ShapeDtypeStruct((RV, views), F32),
            jax.ShapeDtypeStruct((rows, band, RL), F32),
        ),
        in_specs=[vmem] * 5 + [pl.BlockSpec(memory_space=pl.ANY)],
        out_specs=(vmem, vmem, vmem),
        scratch_shapes=[
            pltpu.VMEM((CHUNKS, rows, cut), BF),
            pltpu.VMEM((CHUNKS, tex_count, rows, cut), BF),
            pltpu.VMEM((L, texels, views), BF),
            pltpu.VMEM((L, texels, views), F32),
            pltpu.VMEM((texels, views, L), F32),
            pltpu.VMEM((views, LIGHTS), F32),
            pltpu.VMEM((padded, RV), F32),
            pltpu.VMEM((RV, padded), F32),
            pltpu.VMEM((GROUP * RL, GROUP * LIGHTS), BF),
            pltpu.VMEM((groups, padded, GROUP * RL), BF),
            pltpu.VMEM((groups, padded, GROUP * LIGHTS), BF),
            pltpu.VMEM((CHUNKS, part, texels, RL), F32),
            pltpu.VMEM((CHUNKS, view_count, part, texels * RL), BF),
            pltpu.VMEM((CHUNKS, view_count, part, texels * RL), BF),
            pltpu.VMEM((CHUNKS, peers, part, texels * RL), BF),
            pltpu.VMEM((CHUNKS, part, texels, RL), F32),
            pltpu.VMEM((CHUNKS, texels, cut), BF),
            pltpu.VMEM((texels, RT), F32),
            pltpu.VMEM((peers, texels, RT), F32),
            pltpu.VMEM((steps, RV, padded), F32),
            pltpu.VMEM((steps, RV, padded), F32),
            pltpu.VMEM((CHUNKS, tex_count, rows, cut), BF),
            pltpu.VMEM((CHUNKS, LINE, nb, rows, cut), BF),
            pltpu.VMEM((CHUNKS, LINE, across, rows, cut), BF),
            pltpu.VMEM((CHUNKS, LINE - 1, rows, cut), BF),
            dma, dma((CHUNKS, LINE - 1)), dma((CHUNKS, LINE, across)), dma((CHUNKS, LINE, nb)),
            dma((CHUNKS, tex_count)),
            dma((CHUNKS, peers)), dma((CHUNKS, view_count)),
            dma((CHUNKS, peers)), dma((CHUNKS, peers)),
            dma((peers,)), dma((peers,)), dma((steps,)), dma((steps,)),
            dma((CHUNKS, LINE, nb)), dma((CHUNKS, LINE, nb)),
            dma((CHUNKS, LINE, across)), dma((CHUNKS, LINE, across)),
            dma((CHUNKS, LINE - 1)), dma((CHUNKS, LINE - 1)),
        ],
        compiler_params=pltpu.CompilerParams(
            collective_id=0, has_side_effects=True, vmem_limit_bytes=48 * 1024 * 1024),
        cost_estimate=pl.CostEstimate(flops=10**9, bytes_accessed=10**7, transcendentals=0),
    )(core_tensor, tex_factor, view_factor.T, view_mask.reshape(1, views), light_factor.T,
      jnp.transpose(measured, (2, 0, 1)))
    return tex_new, view_new.T, core_new


def solution(mesh):
    return jax.shard_map(
        per_device,
        mesh=mesh,
        in_specs=(
            P("tex", "view", None),
            P("view"),
            P("tex", None),
            P("view", None),
            P(),
            P("tex", "view", None),
        ),
        out_specs=(P("tex", None), P("view", None), P("tex", "view", None)),
        check_vma=False,
    )
```

```python
import functools

import jax
import jax.numpy as jnp
from jax import lax
from jax.experimental import pallas as pl
from jax.experimental.pallas import tpu as pltpu
from jax.sharding import PartitionSpec as P

RT = 256
RV = 64
RL = 64
VALID = 151
L = 151
LINE = 4
CHUNKS = 2
GROUP = 256 // RL
LIGHTS = 256 * (-(-L // 256))
SCALING = (RT * RV * RL) ** (-0.5)
MESH = pl.DeviceIdType.MESH
BF = jnp.bfloat16
F32 = jnp.float32
NT = (((1,), (1,)), ((), ()))
TN = (((0,), (0,)), ((), ()))


def kernel(
    tex_count, view_count, rates,
    core_hbm, u_hbm, vt_hbm, mask_hbm, lightt_hbm, meas_hbm,
    u_out, vt_out, core_out,
    core_ref, u_ref, vt_ref, mask_ref, lightt_ref, usib, uturn,
    gl, gbuf, meas, mwide, mturn, weights, vcol, vrow, bdw, qbuf, rbuf, p3, pall,
    ysend, yrecv, ysum, yflat, ytot, ysib, us, ur, gvs, gvr, xs, xr, held, zs, zr,
    in_sem, w_s, w_r, ga_s, gb_s, gc_s, g_r, p_s, p_r, y_s, y_r, u_s, u_r, gv_s, gv_r,
    h_s, h_r, x_s, x_r, z_s, z_r,
):
    na = LINE
    nb = tex_count // (2 * na)
    me = lax.axis_index("tex")
    view = lax.axis_index("view")
    core = lax.rem(me, 2)
    b = lax.rem(me // 2, nb)
    a = me // (2 * nb)
    rows, band, _ = core_ref.shape
    part = band // CHUNKS
    texels = u_ref.shape[0]
    views = vt_ref.shape[1]
    padded = vcol.shape[0]
    groups = texels // GROUP
    steps = tex_count.bit_length() - 1
    rate_tex, rate_view, rate_core = rates

    def slot(ai, bi, ci):
        return (ai * nb + bi) * 2 + ci

    def ahead(d):
        return lax.rem(a + d, na)

    def beside(e):
        return lax.rem(b + e, nb)

    def other(w):
        return lax.rem(view + w, view_count)

    sibling = slot(a, b, 1 - core)
    pending = []

    def push(src, dst, ssem, rsem, tex, vw):
        copy = pltpu.make_async_remote_copy(
            src_ref=src, dst_ref=dst, send_sem=ssem, recv_sem=rsem,
            device_id=(tex, vw), device_id_type=MESH,
        )
        copy.start()
        pending.append(copy)

    def arrived(ref, sem):
        pltpu.make_async_copy(ref, ref, sem).wait()

    barrier = pltpu.get_barrier_semaphore()
    peers = [(slot(ahead(d), b, core), view) for d in range(1, na)]
    peers += [(slot(a, beside(e), core), view) for e in range(1, nb)]
    peers += [(sibling, view)]
    peers += [(me, other(w)) for w in range(1, view_count)]
    for peer in peers:
        pl.semaphore_signal(barrier, inc=1, device_id=peer, device_id_type=MESH)
    fetches = [
        pltpu.make_async_copy(src, dst, in_sem.at[i]) for i, (src, dst) in enumerate((
            (core_hbm, core_ref), (u_hbm, u_ref), (meas_hbm, meas),
            (vt_hbm, vt_ref), (mask_hbm, mask_ref), (lightt_hbm, lightt_ref)))
    ]
    for fetch in fetches:
        fetch.start()
    fetches[0].wait()
    for i in range(0, band, 2):
        pair = jnp.concatenate([core_ref[:, i, :], core_ref[:, i + 1, :]], axis=1).astype(BF)
        h, o = divmod(i, part)
        gl[h, :, o * RL:(o + 2) * RL] = pair
    pl.semaphore_wait(barrier, len(peers))

    for h in range(CHUNKS):
        for e in range(1, nb):
            push(gl.at[h], gbuf.at[h, me], gb_s.at[h, 0, e - 1], g_r.at[h, me],
                 slot(a, beside(e), core), view)
        for d in range(1, na):
            push(gl.at[h], gbuf.at[h, me], ga_s.at[h, d - 1], g_r.at[h, me],
                 slot(ahead(d), b, core), view)
        push(gl.at[h], gbuf.at[h, me], gc_s.at[h, 0, 0], g_r.at[h, me], sibling, view)
    fetches[1].wait()
    push(u_ref, usib, w_s, w_r, sibling, view)

    def from_line(h, d):
        s = slot(ahead(na - d), b, core)
        arrived(gbuf.at[h, s], g_r.at[h, s])
        for e in range(1, nb):
            push(gbuf.at[h, s], gbuf.at[h, s], gb_s.at[h, d, e - 1], g_r.at[h, s],
                 slot(a, beside(e), core), view)
        push(gbuf.at[h, s], gbuf.at[h, s], gc_s.at[h, d, 0], g_r.at[h, s], sibling, view)

    def from_across(h):
        for d in range(na):
            for e in range(1, nb):
                s = slot(ahead(na - d), beside(nb - e), core)
                arrived(gbuf.at[h, s], g_r.at[h, s])
                push(gbuf.at[h, s], gbuf.at[h, s], gc_s.at[h, d, e], g_r.at[h, s], sibling, view)

    for h in range(CHUNKS):
        gbuf[h, me] = gl[h]
    bdw[...] = jnp.zeros_like(bdw)
    rbuf[...] = jnp.zeros_like(rbuf)
    for fetch in fetches[2:]:
        fetch.wait()
    for j in range(GROUP):
        bdw[j * RL:(j + 1) * RL, j * LIGHTS:j * LIGHTS + L] = lightt_ref[...]
    vcol[...] = jnp.zeros_like(vcol)
    vrow[...] = jnp.zeros_like(vrow)
    vcol[:views, :] = vt_ref[...].T
    vrow[:, :views] = vt_ref[...]
    weights[...] = jnp.broadcast_to(mask_ref[...].astype(F32), (LIGHTS, views)).T
    mwide[...] = meas[...].astype(F32)
    turns = -(-texels // (CHUNKS * (na - 1)))
    t = 0
    for h in range(CHUNKS):
        for d in range(1, na):
            from_line(h, d)
            for _ in range(turns):
                if t < texels:
                    mturn[t] = mwide[:, t, :].T
                    t += 1

    u_bf = u_ref[...].astype(BF)
    arrived(usib, w_r)
    turned = jnp.concatenate([u_ref[...], usib[...]], axis=0).T
    for j in range(tex_count):
        uturn[j] = turned[j * rows:(j + 1) * rows]

    def stacked(h):
        if rows % 16 == 0:
            return gbuf[h].reshape(tex_count * rows, part * RL)
        return jnp.concatenate(
            [gbuf[h, j].astype(F32) for j in range(tex_count)], axis=0).astype(BF)

    for h in range(CHUNKS):
        from_across(h)
        for ai in range(na):
            for bi in range(nb):
                s = slot(ai, bi, 1 - core)
                arrived(gbuf.at[h, s], g_r.at[h, s])
        proj = jnp.dot(u_bf, stacked(h), preferred_element_type=F32)
        for j in range(part):
            p3[h, j] = proj[:, j * RL:(j + 1) * RL]
        for t in range(0, texels, 2):
            pair = jnp.concatenate([p3[h, :, t, :], p3[h, :, t + 1, :]], axis=1)
            pall[h, view, :, t * RL:(t + 2) * RL] = pair.astype(BF)
        for w in range(1, view_count):
            push(pall.at[h, view], pall.at[h, view], p_s.at[h, w - 1], p_r.at[h, view],
                 me, other(w))
    v_bf = vcol[...].astype(BF)
    vt_bf = vrow[...].astype(BF)
    for h in range(CHUNKS):
        for w in range(1, view_count):
            arrived(pall.at[h, other(w)], p_r.at[h, other(w)])

    def lanes(k):
        return slice(k * GROUP * RL, (k + 1) * GROUP * RL)

    def p_group(k):
        pieces = [pall[h, w, :, lanes(k)] for w in range(view_count) for h in range(CHUNKS)]
        if part % 16 == 0:
            return jnp.concatenate(pieces, axis=0)
        return jnp.concatenate([piece.astype(F32) for piece in pieces], axis=0).astype(BF)

    for k in range(groups):
        qbuf[k] = jnp.dot(v_bf, p_group(k), preferred_element_type=F32).astype(BF)
    q_all = qbuf[...].reshape(groups * padded, GROUP * RL)
    mask = weights[:, :L]
    for j in range(GROUP):
        cols = slice(j * LIGHTS, (j + 1) * LIGHTS)
        approx = jnp.dot(q_all, bdw[:, cols], preferred_element_type=F32)
        for k in range(groups):
            piece = approx[k * padded:k * padded + views, :L]
            resid = mask * (SCALING * piece - mturn[k * GROUP + j])
            rbuf[k, :views, j * LIGHTS:j * LIGHTS + L] = resid.astype(BF)
    r_all = rbuf[...].reshape(groups * padded, GROUP * LIGHTS)
    s_all = lax.dot_general(r_all, bdw[...], NT, preferred_element_type=F32).astype(BF)
    for k in range(groups):
        s4 = s_all[k * padded:(k + 1) * padded]
        y4 = jnp.dot(vt_bf, s4, preferred_element_type=F32).astype(BF)
        for w in range(view_count):
            for h in range(CHUNKS):
                first = w * band + h * part
                ysend[h, w, :, lanes(k)] = y4[first:first + part]
    for h in range(CHUNKS):
        for w in range(1, view_count):
            push(ysend.at[h, other(w)], yrecv.at[h, w - 1], y_s.at[h, w - 1], y_r.at[h, w - 1],
                 me, other(w))
    gv = jnp.zeros((RV, padded), F32)
    for k in range(groups):
        s4 = s_all[k * padded:(k + 1) * padded]
        gv = gv + lax.dot_general(p_group(k), s4, NT, preferred_element_type=F32)

    def gv_start(i, value):
        gvs[i] = value
        partner = me + (1 << i) - 2 * (1 << i) * lax.rem(me // (1 << i), 2)
        push(gvs.at[i], gvr.at[i], gv_s.at[i], gv_r.at[i], partner, view)

    def gv_next(i):
        arrived(gvr.at[i], gv_r.at[i])
        value = gvs[i] + gvr[i]
        if i + 1 < steps:
            gv_start(i + 1, value)
        else:
            vt_out[...] = vt_ref[...] - rate_view * value[:, :views]

    gv_start(0, SCALING * gv)

    order = [d % na for d in range(1, na + 1)]

    def turn(h, first, values):
        for t in range(texels):
            ysum[h, :, first + t, :] = values[:, t * RL:(t + 1) * RL]

    for h in range(CHUNKS):
        total = ysend[h, view].astype(F32)
        for w in range(1, view_count):
            arrived(yrecv.at[h, w - 1], y_r.at[h, w - 1])
            total = total + yrecv[h, w - 1].astype(F32)
        ytot[h] = total.astype(BF)
        push(ytot.at[h], ysib.at[h], h_s.at[h], h_r.at[h], sibling, view)
        turn(h, 0, total)

    def u_rows(e):
        return jnp.concatenate(
            [uturn[slot(ahead(d), beside(e), core)] for d in order], axis=0).astype(BF)

    u_parts = [u_rows(e) for e in range(nb)]
    for h in range(CHUNKS):
        arrived(ysib.at[h], h_r.at[h])
        turn(h, texels, ysib[h].astype(F32))
        for j in range(0, part, 2):
            pair = jnp.concatenate([ysum[h, j], ysum[h, j + 1]], axis=1)
            yflat[h, :, j * RL:(j + 2) * RL] = pair.astype(BF)
        for e in range(1, nb):
            grad = SCALING * jnp.dot(u_parts[e], yflat[h], preferred_element_type=F32)
            for i, d in enumerate(order):
                xs[h, d, e - 1] = grad[i * rows:(i + 1) * rows].astype(BF)
                push(xs.at[h, d, e - 1], xr.at[h, d, e - 1], x_s.at[h, d, e - 1],
                     x_r.at[h, d, e - 1], slot(a, beside(e), core), view)
        grad = SCALING * jnp.dot(u_parts[0], yflat[h], preferred_element_type=F32)
        for i, d in enumerate(order):
            held[h, d] = grad[i * rows:(i + 1) * rows]
        if h == 0:
            gv_next(0)

    partial = jnp.zeros((2 * texels, RT), F32)
    for h in range(CHUNKS):
        partial = partial + lax.dot_general(yflat[h], stacked(h), NT, preferred_element_type=F32)
    us[...] = SCALING * partial[:texels]
    for w in range(1, view_count):
        push(us, ur.at[w - 1], u_s.at[w - 1], u_r.at[w - 1], me, other(w))

    own = []
    for h in range(CHUNKS):
        for d in order:
            block = held[h, d]
            for e in range(1, nb):
                arrived(xr.at[h, d, e - 1], x_r.at[h, d, e - 1])
                block = block + xr[h, d, e - 1].astype(F32)
            if d:
                zs[h, d - 1] = block.astype(BF)
                push(zs.at[h, d - 1], zr.at[h, d - 1], z_s.at[h, d - 1], z_r.at[h, d - 1],
                     slot(ahead(d), b, core), view)
        own.append(block)
        if h + 1 < steps:
            gv_next(h + 1)
    for i in range(CHUNKS + 1, steps):
        gv_next(i)
    total_u = us[...]
    for w in range(1, view_count):
        arrived(ur.at[w - 1], u_r.at[w - 1])
        total_u = total_u + ur[w - 1]
    u_out[...] = u_ref[...] - rate_tex * total_u
    for h in range(CHUNKS):
        block = own[h]
        for d in range(1, na):
            arrived(zr.at[h, d - 1], z_r.at[h, d - 1])
            block = block + zr[h, d - 1].astype(F32)
        block = rate_core * block
        for j in range(part):
            i = h * part + j
            core_out[:, i, :] = core_ref[:, i, :] - block[:, j * RL:(j + 1) * RL]
    for copy in pending:
        copy.wait_send()


def write_out(a_ref, b_ref, c_ref, a_out, b_out, c_out, sems):
    copies = [
        pltpu.make_async_copy(src, dst, sems.at[i])
        for i, (src, dst) in enumerate(((c_ref, c_out), (a_ref, a_out), (b_ref, b_out)))
    ]
    for copy in copies:
        copy.start()
    for copy in copies:
        copy.wait()


def per_device(measured, view_mask, tex_factor, view_factor, light_factor, core_tensor):
    tex_count = lax.axis_size("tex")
    view_count = lax.axis_size("view")
    texels, views, _ = measured.shape
    rows, band, _ = core_tensor.shape
    part = band // CHUNKS
    cut = part * RL
    texels_all = texels * tex_count
    nb = tex_count // (2 * LINE)
    steps = tex_count.bit_length() - 1
    peers = max(view_count - 1, 1)
    across = max(nb - 1, 1)
    padded = 16 * (-(-views // 16))
    groups = texels // GROUP
    rates = (
        RT / (VALID * L),
        RV / (texels_all * L),
        RT * RV * RL / (texels_all * VALID * L),
    )
    vmem = pl.BlockSpec(memory_space=pltpu.VMEM)
    hbm = pl.BlockSpec(memory_space=pltpu.HBM)
    dma = pltpu.SemaphoreType.DMA
    tex_new, view_new, core_new = pl.pallas_call(
        functools.partial(kernel, tex_count, view_count, rates),
        out_shape=(
            jax.ShapeDtypeStruct((texels, RT), F32),
            jax.ShapeDtypeStruct((RV, views), F32),
            jax.ShapeDtypeStruct((rows, band, RL), F32),
        ),
        in_specs=[hbm] * 6,
        out_specs=(vmem, vmem, vmem),
        scratch_shapes=[
            pltpu.VMEM((rows, band, RL), F32),
            pltpu.VMEM((texels, RT), F32),
            pltpu.VMEM((RV, views), F32),
            pltpu.VMEM((1, views), jnp.int32),
            pltpu.VMEM((RL, L), BF),
            pltpu.VMEM((texels, RT), F32),
            pltpu.VMEM((tex_count, rows, 2 * texels), F32),
            pltpu.VMEM((CHUNKS, rows, cut), BF),
            pltpu.VMEM((CHUNKS, tex_count, rows, cut), BF),
            pltpu.VMEM((L, texels, views), BF),
            pltpu.VMEM((L, texels, views), F32),
            pltpu.VMEM((texels, views, L), F32),
            pltpu.VMEM((views, LIGHTS), F32),
            pltpu.VMEM((padded, RV), F32),
            pltpu.VMEM((RV, padded), F32),
            pltpu.VMEM((GROUP * RL, GROUP * LIGHTS), BF),
            pltpu.VMEM((groups, padded, GROUP * RL), BF),
            pltpu.VMEM((groups, padded, GROUP * LIGHTS), BF),
            pltpu.VMEM((CHUNKS, part, texels, RL), F32),
            pltpu.VMEM((CHUNKS, view_count, part, texels * RL), BF),
            pltpu.VMEM((CHUNKS, view_count, part, texels * RL), BF),
            pltpu.VMEM((CHUNKS, peers, part, texels * RL), BF),
            pltpu.VMEM((CHUNKS, part, 2 * texels, RL), F32),
            pltpu.VMEM((CHUNKS, 2 * texels, cut), BF),
            pltpu.VMEM((CHUNKS, part, texels * RL), BF),
            pltpu.VMEM((CHUNKS, part, texels * RL), BF),
            pltpu.VMEM((texels, RT), F32),
            pltpu.VMEM((peers, texels, RT), F32),
            pltpu.VMEM((steps, RV, padded), F32),
            pltpu.VMEM((steps, RV, padded), F32),
            pltpu.VMEM((CHUNKS, LINE, across, rows, cut), BF),
            pltpu.VMEM((CHUNKS, LINE, across, rows, cut), BF),
            pltpu.VMEM((CHUNKS, LINE, rows, cut), F32),
            pltpu.VMEM((CHUNKS, LINE - 1, rows, cut), BF),
            pltpu.VMEM((CHUNKS, LINE - 1, rows, cut), BF),
            dma((6,)), dma, dma, dma((CHUNKS, LINE - 1)), dma((CHUNKS, LINE, across)), dma((CHUNKS, LINE, nb)),
            dma((CHUNKS, tex_count)),
            dma((CHUNKS, peers)), dma((CHUNKS, view_count)),
            dma((CHUNKS, peers)), dma((CHUNKS, peers)),
            dma((peers,)), dma((peers,)), dma((steps,)), dma((steps,)),
            dma((CHUNKS,)), dma((CHUNKS,)),
            dma((CHUNKS, LINE, across)), dma((CHUNKS, LINE, across)),
            dma((CHUNKS, LINE - 1)), dma((CHUNKS, LINE - 1)),
        ],
        compiler_params=pltpu.CompilerParams(
            collective_id=0, has_side_effects=True, vmem_limit_bytes=48 * 1024 * 1024),
        cost_estimate=pl.CostEstimate(flops=10**9, bytes_accessed=10**7, transcendentals=0),
    )(*(pltpu.with_memory_space_constraint(x, pltpu.HBM) for x in (
        core_tensor, tex_factor, view_factor.T, view_mask.reshape(1, views), light_factor.T,
        jnp.transpose(measured, (2, 0, 1)))))
    tex_new, view_new, core_new = pl.pallas_call(
        write_out,
        out_shape=(
            jax.ShapeDtypeStruct((texels, RT), F32),
            jax.ShapeDtypeStruct((RV, views), F32),
            jax.ShapeDtypeStruct((rows, band, RL), F32),
        ),
        in_specs=[vmem] * 3,
        out_specs=(hbm, hbm, hbm),
        scratch_shapes=[dma((3,))],
    )(tex_new, view_new, core_new)
    return tex_new, view_new.T, core_new


def solution(mesh):
    return jax.shard_map(
        per_device,
        mesh=mesh,
        in_specs=(
            P("tex", "view", None),
            P("view"),
            P("tex", None),
            P("view", None),
            P(),
            P("tex", "view", None),
        ),
        out_specs=(P("tex", None), P("view", None), P("tex", "view", None)),
        check_vma=False,
    )
```

```python
import functools

import jax
import jax.numpy as jnp
from jax import lax
from jax.experimental import pallas as pl
from jax.experimental.pallas import tpu as pltpu
from jax.sharding import PartitionSpec as P

RT = 256
RV = 64
RL = 64
VALID = 151
L = 151
LINE = 4
CHUNKS = 2
GROUP = 256 // RL
LIGHTS = 256 * (-(-L // 256))
SCALING = (RT * RV * RL) ** (-0.5)
MESH = pl.DeviceIdType.MESH
BF = jnp.bfloat16
F32 = jnp.float32
NT = (((1,), (1,)), ((), ()))
TN = (((0,), (0,)), ((), ()))


def kernel(
    tex_count, view_count, rates,
    core_hbm, u_hbm, vt_hbm, mask_hbm, lightt_hbm, meas_hbm,
    u_hbm_out, vt_hbm_out, core_hbm_out,
    u_out, vt_out, core_out, out_sem,
    core_ref, u_ref, vt_ref, mask_ref, lightt_ref, usib, uturn, uown,
    gl, gbuf, meas, mwide, mturn, weights, vcol, vrow, bdw, qbuf, rbuf, psend, psib, p3, pall,
    ysend, yrecv, ysum, yflat, ytot, ysib, us, ubuf, gvs, gvr, xs, xr, held, zs, zr,
    in_sem, w_s, w_r, ga_s, gb_s, g_r, q_s, q_r, p_s, p_r, y_s, y_r, u_s, u_r, gv_s, gv_r,
    h_s, h_r, x_s, x_r, z_s, z_r,
):
    na = LINE
    nb = tex_count // (2 * na)
    me = lax.axis_index("tex")
    view = lax.axis_index("view")
    core = lax.rem(me, 2)
    b = lax.rem(me // 2, nb)
    a = me // (2 * nb)
    rows, band, _ = core_ref.shape
    part = band // CHUNKS
    texels = u_ref.shape[0]
    views = vt_ref.shape[1]
    padded = vcol.shape[0]
    groups = texels // GROUP
    steps = tex_count.bit_length() - 1
    rate_tex, rate_view, rate_core = rates

    def slot(ai, bi, ci):
        return (ai * nb + bi) * 2 + ci

    def ahead(d):
        return lax.rem(a + d, na)

    def beside(e):
        return lax.rem(b + e, nb)

    def other(w):
        return lax.rem(view + w, view_count)

    sibling = slot(a, b, 1 - core)
    pending = []

    def push(src, dst, ssem, rsem, tex, vw):
        copy = pltpu.make_async_remote_copy(
            src_ref=src, dst_ref=dst, send_sem=ssem, recv_sem=rsem,
            device_id=(tex, vw), device_id_type=MESH,
        )
        copy.start()
        pending.append(copy)

    def arrived(ref, sem):
        pltpu.make_async_copy(ref, ref, sem).wait()

    barrier = pltpu.get_barrier_semaphore()
    peers = [(slot(ahead(d), b, core), view) for d in range(1, na)]
    peers += [(slot(a, beside(e), core), view) for e in range(1, nb)]
    peers += [(sibling, view)]
    peers += [(tex, other(w)) for w in range(1, view_count) for tex in (me, sibling)]
    for peer in peers:
        pl.semaphore_signal(barrier, inc=1, device_id=peer, device_id_type=MESH)
    fetches = [
        pltpu.make_async_copy(src, dst, in_sem.at[i]) for i, (src, dst) in enumerate((
            (core_hbm, core_ref), (u_hbm, u_ref), (meas_hbm, meas),
            (vt_hbm, vt_ref), (mask_hbm, mask_ref), (lightt_hbm, lightt_ref)))
    ]
    for fetch in fetches:
        fetch.start()
    fetches[0].wait()
    for i in range(0, band, 2):
        pair = jnp.concatenate([core_ref[:, i, :], core_ref[:, i + 1, :]], axis=1).astype(BF)
        h, o = divmod(i, part)
        gl[h, :, o * RL:(o + 2) * RL] = pair
    pl.semaphore_wait(barrier, len(peers))

    for h in range(CHUNKS):
        for e in range(1, nb):
            push(gl.at[h], gbuf.at[h, a, b], gb_s.at[h, 0, e - 1], g_r.at[h, a, b],
                 slot(a, beside(e), core), view)
        for d in range(1, na):
            push(gl.at[h], gbuf.at[h, a, b], ga_s.at[h, d - 1], g_r.at[h, a, b],
                 slot(ahead(d), b, core), view)
    fetches[1].wait()
    push(u_ref, usib, w_s, w_r, sibling, view)

    def from_line(h, d):
        ad = ahead(na - d)
        arrived(gbuf.at[h, ad, b], g_r.at[h, ad, b])
        for e in range(1, nb):
            push(gbuf.at[h, ad, b], gbuf.at[h, ad, b], gb_s.at[h, d, e - 1], g_r.at[h, ad, b],
                 slot(a, beside(e), core), view)

    def from_across(h):
        for d in range(na):
            for e in range(1, nb):
                ad, be = ahead(na - d), beside(nb - e)
                arrived(gbuf.at[h, ad, be], g_r.at[h, ad, be])

    for h in range(CHUNKS):
        gbuf[h, a, b] = gl[h]
    bdw[...] = jnp.zeros_like(bdw)
    rbuf[...] = jnp.zeros_like(rbuf)
    for fetch in fetches[2:]:
        fetch.wait()
    for j in range(GROUP):
        bdw[j * RL:(j + 1) * RL, j * LIGHTS:j * LIGHTS + L] = lightt_ref[...]
    vcol[...] = jnp.zeros_like(vcol)
    vrow[...] = jnp.zeros_like(vrow)
    vcol[:views, :] = vt_ref[...].T
    vrow[:, :views] = vt_ref[...]
    weights[...] = jnp.broadcast_to(mask_ref[...].astype(F32), (LIGHTS, views)).T
    mwide[...] = meas[...].astype(F32)
    turns = texels // (2 * CHUNKS * (na - 1))
    t = 0
    for h in range(CHUNKS):
        for d in range(1, na):
            from_line(h, d)
            for _ in range(turns):
                mturn[t] = mwide[:, t, :].T
                t += 1
    while t < texels:
        mturn[t] = mwide[:, t, :].T
        t += 1

    arrived(usib, w_r)
    turned = jnp.concatenate([u_ref[...], usib[...]], axis=0).T
    for j in range(tex_count):
        uturn[j] = turned[j * rows:(j + 1) * rows]
    pairs = [(ai, bi) for ai in range(na) for bi in range(nb)]
    uown[...] = jnp.concatenate([uturn[slot(ai, bi, core)] for ai, bi in pairs], axis=0).T.astype(BF)
    u_own = uown[...]

    def stacked(h):
        if rows % 16 == 0:
            return gbuf[h].reshape(len(pairs) * rows, part * RL)
        return jnp.concatenate(
            [gbuf[h, ai, bi].astype(F32) for ai, bi in pairs], axis=0).astype(BF)

    kept = []
    for h in range(CHUNKS):
        from_across(h)
        proj = jnp.dot(u_own, stacked(h), preferred_element_type=F32)
        psend[h] = proj[texels:]
        push(psend.at[h], psib.at[h], q_s.at[h], q_r.at[h], sibling, view)
        kept.append(proj[:texels])
    for h in range(CHUNKS):
        arrived(psib.at[h], q_r.at[h])
        proj = kept[h] + psib[h]
        for j in range(part):
            p3[h, j] = proj[:, j * RL:(j + 1) * RL]
        for t in range(0, texels, 2):
            pair = jnp.concatenate([p3[h, :, t, :], p3[h, :, t + 1, :]], axis=1)
            pall[h, view, :, t * RL:(t + 2) * RL] = pair.astype(BF)
        for w in range(1, view_count):
            push(pall.at[h, view], pall.at[h, view], p_s.at[h, w - 1], p_r.at[h, view],
                 me, other(w))
    v_bf = vcol[...].astype(BF)
    vt_bf = vrow[...].astype(BF)
    for h in range(CHUNKS):
        for w in range(1, view_count):
            arrived(pall.at[h, other(w)], p_r.at[h, other(w)])

    def lanes(k):
        return slice(k * GROUP * RL, (k + 1) * GROUP * RL)

    def p_group(k):
        pieces = [pall[h, w, :, lanes(k)] for w in range(view_count) for h in range(CHUNKS)]
        if part % 16 == 0:
            return jnp.concatenate(pieces, axis=0)
        return jnp.concatenate([piece.astype(F32) for piece in pieces], axis=0).astype(BF)

    for k in range(groups):
        qbuf[k] = jnp.dot(v_bf, p_group(k), preferred_element_type=F32).astype(BF)
    q_all = qbuf[...].reshape(groups * padded, GROUP * RL)
    mask = weights[:, :L]
    for j in range(GROUP):
        cols = slice(j * LIGHTS, (j + 1) * LIGHTS)
        approx = jnp.dot(q_all, bdw[:, cols], preferred_element_type=F32)
        for k in range(groups):
            piece = approx[k * padded:k * padded + views, :L]
            resid = mask * (SCALING * piece - mturn[k * GROUP + j])
            rbuf[k, :views, j * LIGHTS:j * LIGHTS + L] = resid.astype(BF)
    r_all = rbuf[...].reshape(groups * padded, GROUP * LIGHTS)
    s_all = lax.dot_general(r_all, bdw[...], NT, preferred_element_type=F32).astype(BF)
    for k in range(groups):
        s4 = s_all[k * padded:(k + 1) * padded]
        y4 = jnp.dot(vt_bf, s4, preferred_element_type=F32).astype(BF)
        for w in range(view_count):
            for h in range(CHUNKS):
                first = w * band + h * part
                ysend[h, w, :, lanes(k)] = y4[first:first + part]
    for h in range(CHUNKS):
        for w in range(1, view_count):
            push(ysend.at[h, other(w)], yrecv.at[h, w - 1], y_s.at[h, w - 1], y_r.at[h, w - 1],
                 me, other(w))
    gv = jnp.zeros((RV, padded), F32)
    for k in range(groups):
        s4 = s_all[k * padded:(k + 1) * padded]
        gv = gv + lax.dot_general(p_group(k), s4, NT, preferred_element_type=F32)

    results = [
        pltpu.make_async_copy(src, dst, out_sem.at[i]) for i, (src, dst) in enumerate((
            (u_out, u_hbm_out), (vt_out, vt_hbm_out), (core_out, core_hbm_out)))
    ]

    def gv_start(i, value):
        gvs[i] = value
        partner = me + (1 << i) - 2 * (1 << i) * lax.rem(me // (1 << i), 2)
        push(gvs.at[i], gvr.at[i], gv_s.at[i], gv_r.at[i], partner, view)

    def gv_next(i):
        arrived(gvr.at[i], gv_r.at[i])
        value = gvs[i] + gvr[i]
        if i + 1 < steps:
            gv_start(i + 1, value)
        else:
            vt_out[...] = vt_ref[...] - rate_view * value[:, :views]
            results[1].start()

    gv_start(0, SCALING * gv)

    order = [d % na for d in range(1, na + 1)]

    def turn(h, first, values):
        for t in range(texels):
            ysum[h, :, first + t, :] = values[:, t * RL:(t + 1) * RL]

    for h in range(CHUNKS):
        total = ysend[h, view].astype(F32)
        for w in range(1, view_count):
            arrived(yrecv.at[h, w - 1], y_r.at[h, w - 1])
            total = total + yrecv[h, w - 1].astype(F32)
        ytot[h] = total.astype(BF)
        push(ytot.at[h], ysib.at[h], h_s.at[h], h_r.at[h], sibling, view)
        turn(h, 0, total)

    def u_rows(e):
        return jnp.concatenate(
            [uturn[slot(ahead(d), beside(e), core)] for d in order], axis=0).astype(BF)

    u_parts = [u_rows(e) for e in range(nb)]
    for h in range(CHUNKS):
        arrived(ysib.at[h], h_r.at[h])
        turn(h, texels, ysib[h].astype(F32))
        for j in range(0, part, 2):
            pair = jnp.concatenate([ysum[h, j], ysum[h, j + 1]], axis=1)
            yflat[h, :, j * RL:(j + 2) * RL] = pair.astype(BF)
        for e in range(1, nb):
            grad = SCALING * jnp.dot(u_parts[e], yflat[h], preferred_element_type=F32)
            for i, d in enumerate(order):
                xs[h, d, e - 1] = grad[i * rows:(i + 1) * rows].astype(BF)
                push(xs.at[h, d, e - 1], xr.at[h, d, e - 1], x_s.at[h, d, e - 1],
                     x_r.at[h, d, e - 1], slot(a, beside(e), core), view)
        grad = SCALING * jnp.dot(u_parts[0], yflat[h], preferred_element_type=F32)
        for i, d in enumerate(order):
            held[h, d] = grad[i * rows:(i + 1) * rows]
        if h == 0:
            gv_next(0)

    partial = jnp.zeros((2 * texels, RT // 2), F32)
    for h in range(CHUNKS):
        partial = partial + lax.dot_general(yflat[h], stacked(h), NT, preferred_element_type=F32)
    us[0] = SCALING * partial[:texels]
    us[1] = SCALING * partial[texels:]
    ubuf[view, core] = us[0]
    targets = [(1, sibling, view)]
    for w in range(1, view_count):
        targets += [(0, me, other(w)), (1, sibling, other(w))]
    for i, (half, tex, vw) in enumerate(targets):
        push(us.at[half], ubuf.at[view, core], u_s.at[i], u_r.at[view, core], tex, vw)

    own = []
    for h in range(CHUNKS):
        for d in order:
            block = held[h, d]
            for e in range(1, nb):
                arrived(xr.at[h, d, e - 1], x_r.at[h, d, e - 1])
                block = block + xr[h, d, e - 1].astype(F32)
            if d:
                zs[h, d - 1] = block.astype(BF)
                push(zs.at[h, d - 1], zr.at[h, d - 1], z_s.at[h, d - 1], z_r.at[h, d - 1],
                     slot(ahead(d), b, core), view)
        own.append(block)
        if h + 1 < steps:
            gv_next(h + 1)
    for i in range(CHUNKS + 1, steps):
        gv_next(i)
    arrived(ubuf.at[view, 1 - core], u_r.at[view, 1 - core])
    for w in range(1, view_count):
        for ci in range(2):
            arrived(ubuf.at[other(w), ci], u_r.at[other(w), ci])
    halves = [sum(ubuf[w, ci] for w in range(view_count)).T for ci in range(2)]
    total_u = jnp.concatenate(
        [halves[j % 2][j // 2 * rows:(j // 2 + 1) * rows] for j in range(tex_count)], axis=0).T
    u_out[...] = u_ref[...] - rate_tex * total_u
    results[0].start()
    for h in range(CHUNKS):
        block = own[h]
        for d in range(1, na):
            arrived(zr.at[h, d - 1], z_r.at[h, d - 1])
            block = block + zr[h, d - 1].astype(F32)
        block = rate_core * block
        for j in range(part):
            i = h * part + j
            core_out[:, i, :] = core_ref[:, i, :] - block[:, j * RL:(j + 1) * RL]
    results[2].start()
    for copy in pending:
        copy.wait_send()
    for result in results:
        result.wait()


def write_out(a_ref, b_ref, c_ref, a_out, b_out, c_out, sems):
    copies = [
        pltpu.make_async_copy(src, dst, sems.at[i])
        for i, (src, dst) in enumerate(((c_ref, c_out), (a_ref, a_out), (b_ref, b_out)))
    ]
    for copy in copies:
        copy.start()
    for copy in copies:
        copy.wait()


def per_device(measured, view_mask, tex_factor, view_factor, light_factor, core_tensor):
    tex_count = lax.axis_size("tex")
    view_count = lax.axis_size("view")
    texels, views, _ = measured.shape
    rows, band, _ = core_tensor.shape
    part = band // CHUNKS
    cut = part * RL
    texels_all = texels * tex_count
    nb = tex_count // (2 * LINE)
    steps = tex_count.bit_length() - 1
    peers = max(view_count - 1, 1)
    across = max(nb - 1, 1)
    padded = 16 * (-(-views // 16))
    groups = texels // GROUP
    rates = (
        RT / (VALID * L),
        RV / (texels_all * L),
        RT * RV * RL / (texels_all * VALID * L),
    )
    hbm = pl.BlockSpec(memory_space=pltpu.HBM)
    dma = pltpu.SemaphoreType.DMA
    tex_new, view_new, core_new = pl.pallas_call(
        functools.partial(kernel, tex_count, view_count, rates),
        out_shape=(
            jax.ShapeDtypeStruct((texels, RT), F32),
            jax.ShapeDtypeStruct((RV, views), F32),
            jax.ShapeDtypeStruct((rows, band, RL), F32),
        ),
        in_specs=[hbm] * 6,
        out_specs=(hbm, hbm, hbm),
        scratch_shapes=[
            pltpu.VMEM((texels, RT), F32),
            pltpu.VMEM((RV, views), F32),
            pltpu.VMEM((rows, band, RL), F32),
            dma((3,)),
            pltpu.VMEM((rows, band, RL), F32),
            pltpu.VMEM((texels, RT), F32),
            pltpu.VMEM((RV, views), F32),
            pltpu.VMEM((1, views), jnp.int32),
            pltpu.VMEM((RL, L), BF),
            pltpu.VMEM((texels, RT), F32),
            pltpu.VMEM((tex_count, rows, 2 * texels), F32),
            pltpu.VMEM((2 * texels, RT // 2), BF),
            pltpu.VMEM((CHUNKS, rows, cut), BF),
            pltpu.VMEM((CHUNKS, LINE, nb, rows, cut), BF),
            pltpu.VMEM((L, texels, views), BF),
            pltpu.VMEM((L, texels, views), F32),
            pltpu.VMEM((texels, views, L), F32),
            pltpu.VMEM((views, LIGHTS), F32),
            pltpu.VMEM((padded, RV), F32),
            pltpu.VMEM((RV, padded), F32),
            pltpu.VMEM((GROUP * RL, GROUP * LIGHTS), BF),
            pltpu.VMEM((groups, padded, GROUP * RL), BF),
            pltpu.VMEM((groups, padded, GROUP * LIGHTS), BF),
            pltpu.VMEM((CHUNKS, texels, cut), F32),
            pltpu.VMEM((CHUNKS, texels, cut), F32),
            pltpu.VMEM((CHUNKS, part, texels, RL), F32),
            pltpu.VMEM((CHUNKS, view_count, part, texels * RL), BF),
            pltpu.VMEM((CHUNKS, view_count, part, texels * RL), BF),
            pltpu.VMEM((CHUNKS, peers, part, texels * RL), BF),
            pltpu.VMEM((CHUNKS, part, 2 * texels, RL), F32),
            pltpu.VMEM((CHUNKS, 2 * texels, cut), BF),
            pltpu.VMEM((CHUNKS, part, texels * RL), BF),
            pltpu.VMEM((CHUNKS, part, texels * RL), BF),
            pltpu.VMEM((2, texels, RT // 2), F32),
            pltpu.VMEM((view_count, 2, texels, RT // 2), F32),
            pltpu.VMEM((steps, RV, padded), F32),
            pltpu.VMEM((steps, RV, padded), F32),
            pltpu.VMEM((CHUNKS, LINE, across, rows, cut), BF),
            pltpu.VMEM((CHUNKS, LINE, across, rows, cut), BF),
            pltpu.VMEM((CHUNKS, LINE, rows, cut), F32),
            pltpu.VMEM((CHUNKS, LINE - 1, rows, cut), BF),
            pltpu.VMEM((CHUNKS, LINE - 1, rows, cut), BF),
            dma((6,)), dma, dma, dma((CHUNKS, LINE - 1)), dma((CHUNKS, LINE, across)),
            dma((CHUNKS, LINE, nb)), dma((CHUNKS,)), dma((CHUNKS,)),
            dma((CHUNKS, peers)), dma((CHUNKS, view_count)),
            dma((CHUNKS, peers)), dma((CHUNKS, peers)),
            dma((2 * peers + 1,)), dma((view_count, 2)), dma((steps,)), dma((steps,)),
            dma((CHUNKS,)), dma((CHUNKS,)),
            dma((CHUNKS, LINE, across)), dma((CHUNKS, LINE, across)),
            dma((CHUNKS, LINE - 1)), dma((CHUNKS, LINE - 1)),
        ],
        compiler_params=pltpu.CompilerParams(
            collective_id=0, has_side_effects=True, vmem_limit_bytes=48 * 1024 * 1024),
        cost_estimate=pl.CostEstimate(flops=10**9, bytes_accessed=10**7, transcendentals=0),
    )(*(pltpu.with_memory_space_constraint(x, pltpu.HBM) for x in (
        core_tensor, tex_factor, view_factor.T, view_mask.reshape(1, views), light_factor.T,
        jnp.transpose(measured, (2, 0, 1)))))
    tex_new, view_new, core_new = pl.pallas_call(
        write_out,
        out_shape=(
            jax.ShapeDtypeStruct((texels, RT), F32),
            jax.ShapeDtypeStruct((RV, views), F32),
            jax.ShapeDtypeStruct((rows, band, RL), F32),
        ),
        in_specs=[hbm] * 3,
        out_specs=(hbm, hbm, hbm),
        scratch_shapes=[dma((3,))],
    )(*(pltpu.with_memory_space_constraint(x, pltpu.HBM) for x in (tex_new, view_new, core_new)))
    return tex_new, view_new.T, core_new


def solution(mesh):
    return jax.shard_map(
        per_device,
        mesh=mesh,
        in_specs=(
            P("tex", "view", None),
            P("view"),
            P("tex", None),
            P("view", None),
            P(),
            P("tex", "view", None),
        ),
        out_specs=(P("tex", None), P("view", None), P("tex", "view", None)),
        check_vma=False,
    )
```

```python
import functools

import jax
import jax.numpy as jnp
from jax import lax
from jax.experimental import pallas as pl
from jax.experimental.pallas import tpu as pltpu
from jax.sharding import PartitionSpec as P

RT = 256
RV = 64
RL = 64
VALID = 151
L = 151
LINE = 4
CHUNKS = 2
GROUP = 256 // RL
LIGHTS = 256 * (-(-L // 256))
SCALING = (RT * RV * RL) ** (-0.5)
MESH = pl.DeviceIdType.MESH
BF = jnp.bfloat16
F32 = jnp.float32
NT = (((1,), (1,)), ((), ()))
TN = (((0,), (0,)), ((), ()))


def kernel(
    tex_count, view_count, rates,
    core_hbm, u_hbm, vt_hbm, mask_hbm, lightt_hbm, meas_hbm,
    u_out, vt_out, core_out,
    core_ref, u_ref, vt_ref, mask_ref, lightt_ref, usib, uturn, uown,
    gl, gbuf, meas, mwide, mturn, weights, vcol, vrow, bdw, qbuf, rbuf, psend, psib, p3, pall,
    ysend, yrecv, ysum, yflat, ytot, ysib, us, ubuf, gvs, gvr, xs, xr, held, zs, zr,
    in_sem, w_s, w_r, ga_s, gb_s, g_r, q_s, q_r, p_s, p_r, y_s, y_r, u_s, u_r, gv_s, gv_r,
    h_s, h_r, x_s, x_r, z_s, z_r,
):
    na = LINE
    nb = tex_count // (2 * na)
    me = lax.axis_index("tex")
    view = lax.axis_index("view")
    core = lax.rem(me, 2)
    b = lax.rem(me // 2, nb)
    a = me // (2 * nb)
    _, rows, cut = gl.shape
    part = cut // RL
    band = part * CHUNKS
    texels = u_ref.shape[0]
    views = vt_ref.shape[1]
    padded = vcol.shape[0]
    groups = texels // GROUP
    steps = tex_count.bit_length() - 1
    rate_tex, rate_view, rate_core = rates

    def slot(ai, bi, ci):
        return (ai * nb + bi) * 2 + ci

    def ahead(d):
        return lax.rem(a + d, na)

    def beside(e):
        return lax.rem(b + e, nb)

    def other(w):
        return lax.rem(view + w, view_count)

    sibling = slot(a, b, 1 - core)
    pending = []

    def push(src, dst, ssem, rsem, tex, vw):
        copy = pltpu.make_async_remote_copy(
            src_ref=src, dst_ref=dst, send_sem=ssem, recv_sem=rsem,
            device_id=(tex, vw), device_id_type=MESH,
        )
        copy.start()
        pending.append(copy)

    def arrived(ref, sem):
        pltpu.make_async_copy(ref, ref, sem).wait()

    barrier = pltpu.get_barrier_semaphore()
    peers = [(slot(ahead(d), b, core), view) for d in range(1, na)]
    peers += [(slot(a, beside(e), core), view) for e in range(1, nb)]
    peers += [(sibling, view)]
    peers += [(tex, other(w)) for w in range(1, view_count) for tex in (me, sibling)]
    for peer in peers:
        pl.semaphore_signal(barrier, inc=1, device_id=peer, device_id_type=MESH)
    fetches = [
        pltpu.make_async_copy(src, dst, in_sem.at[i]) for i, (src, dst) in enumerate((
            (core_hbm, core_ref), (u_hbm, u_ref), (meas_hbm, meas),
            (vt_hbm, vt_ref), (mask_hbm, mask_ref), (lightt_hbm, lightt_ref)))
    ]
    for fetch in fetches:
        fetch.start()
    fetches[0].wait()
    for i in range(0, band, 2):
        pair = jnp.concatenate(
            [core_ref[pl.ds(i + k, rows, stride=band), :] for k in range(2)], axis=1).astype(BF)
        h, o = divmod(i, part)
        gl[h, :, o * RL:(o + 2) * RL] = pair
    pl.semaphore_wait(barrier, len(peers))

    for h in range(CHUNKS):
        for e in range(1, nb):
            push(gl.at[h], gbuf.at[h, a, b], gb_s.at[h, 0, e - 1], g_r.at[h, a, b],
                 slot(a, beside(e), core), view)
        for d in range(1, na):
            push(gl.at[h], gbuf.at[h, a, b], ga_s.at[h, d - 1], g_r.at[h, a, b],
                 slot(ahead(d), b, core), view)
    fetches[1].wait()
    push(u_ref, usib, w_s, w_r, sibling, view)

    def from_line(h, d):
        ad = ahead(na - d)
        arrived(gbuf.at[h, ad, b], g_r.at[h, ad, b])
        for e in range(1, nb):
            push(gbuf.at[h, ad, b], gbuf.at[h, ad, b], gb_s.at[h, d, e - 1], g_r.at[h, ad, b],
                 slot(a, beside(e), core), view)

    def from_across(h):
        for d in range(na):
            for e in range(1, nb):
                ad, be = ahead(na - d), beside(nb - e)
                arrived(gbuf.at[h, ad, be], g_r.at[h, ad, be])

    for h in range(CHUNKS):
        gbuf[h, a, b] = gl[h]
    bdw[...] = jnp.zeros_like(bdw)
    rbuf[...] = jnp.zeros_like(rbuf)
    for fetch in fetches[2:]:
        fetch.wait()
    for j in range(GROUP):
        bdw[j * RL:(j + 1) * RL, j * LIGHTS:j * LIGHTS + L] = lightt_ref[...]
    vcol[...] = jnp.zeros_like(vcol)
    vrow[...] = jnp.zeros_like(vrow)
    vcol[:views, :] = vt_ref[...].T
    vrow[:, :views] = vt_ref[...]
    weights[...] = jnp.broadcast_to(mask_ref[...].astype(F32), (LIGHTS, views)).T
    mwide[...] = meas[...].astype(F32).reshape(mwide.shape)
    turns = texels // (2 * CHUNKS * (na - 1))
    t = 0
    for h in range(CHUNKS):
        for d in range(1, na):
            from_line(h, d)
            for _ in range(turns):
                mturn[t] = mwide[pl.ds(t, L, stride=texels), :].T
                t += 1
    while t < texels:
        mturn[t] = mwide[pl.ds(t, L, stride=texels), :].T
        t += 1

    arrived(usib, w_r)
    turned = jnp.concatenate([u_ref[...], usib[...]], axis=0).T
    for j in range(tex_count):
        uturn[j] = turned[j * rows:(j + 1) * rows]
    pairs = [(ai, bi) for ai in range(na) for bi in range(nb)]
    uown[...] = jnp.concatenate([uturn[slot(ai, bi, core)] for ai, bi in pairs], axis=0).T.astype(BF)
    u_own = uown[...]

    def stacked(h):
        if rows % 16 == 0:
            return gbuf[h].reshape(len(pairs) * rows, part * RL)
        return jnp.concatenate(
            [gbuf[h, ai, bi].astype(F32) for ai, bi in pairs], axis=0).astype(BF)

    kept = []
    for h in range(CHUNKS):
        from_across(h)
        proj = jnp.dot(u_own, stacked(h), preferred_element_type=F32)
        psend[h] = proj[texels:]
        push(psend.at[h], psib.at[h], q_s.at[h], q_r.at[h], sibling, view)
        kept.append(proj[:texels])
    for h in range(CHUNKS):
        arrived(psib.at[h], q_r.at[h])
        proj = kept[h] + psib[h]
        for j in range(part):
            p3[h, j * texels:(j + 1) * texels, :] = proj[:, j * RL:(j + 1) * RL]
        for t in range(0, texels, 2):
            pair = jnp.concatenate(
                [p3[h, pl.ds(t + k, part, stride=texels), :] for k in range(2)], axis=1)
            pall[h, view, :, t * RL:(t + 2) * RL] = pair.astype(BF)
        for w in range(1, view_count):
            push(pall.at[h, view], pall.at[h, view], p_s.at[h, w - 1], p_r.at[h, view],
                 me, other(w))
    v_bf = vcol[...].astype(BF)
    vt_bf = vrow[...].astype(BF)
    for h in range(CHUNKS):
        for w in range(1, view_count):
            arrived(pall.at[h, other(w)], p_r.at[h, other(w)])

    def lanes(k):
        return slice(k * GROUP * RL, (k + 1) * GROUP * RL)

    def p_group(k):
        pieces = [pall[h, w, :, lanes(k)] for w in range(view_count) for h in range(CHUNKS)]
        if part % 16 == 0:
            return jnp.concatenate(pieces, axis=0)
        return jnp.concatenate([piece.astype(F32) for piece in pieces], axis=0).astype(BF)

    for k in range(groups):
        qbuf[k] = jnp.dot(v_bf, p_group(k), preferred_element_type=F32).astype(BF)
    q_all = qbuf[...].reshape(groups * padded, GROUP * RL)
    mask = weights[:, :L]
    for j in range(GROUP):
        cols = slice(j * LIGHTS, (j + 1) * LIGHTS)
        approx = jnp.dot(q_all, bdw[:, cols], preferred_element_type=F32)
        for k in range(groups):
            piece = approx[k * padded:k * padded + views, :L]
            resid = mask * (SCALING * piece - mturn[k * GROUP + j])
            rbuf[k, :views, j * LIGHTS:j * LIGHTS + L] = resid.astype(BF)
    r_all = rbuf[...].reshape(groups * padded, GROUP * LIGHTS)
    s_all = lax.dot_general(r_all, bdw[...], NT, preferred_element_type=F32).astype(BF)
    for k in range(groups):
        s4 = s_all[k * padded:(k + 1) * padded]
        y4 = jnp.dot(vt_bf, s4, preferred_element_type=F32).astype(BF)
        for w in range(view_count):
            for h in range(CHUNKS):
                first = w * band + h * part
                ysend[h, w, :, lanes(k)] = y4[first:first + part]
    for h in range(CHUNKS):
        for w in range(1, view_count):
            push(ysend.at[h, other(w)], yrecv.at[h, w - 1], y_s.at[h, w - 1], y_r.at[h, w - 1],
                 me, other(w))
    gv = jnp.zeros((RV, padded), F32)
    for k in range(groups):
        s4 = s_all[k * padded:(k + 1) * padded]
        gv = gv + lax.dot_general(p_group(k), s4, NT, preferred_element_type=F32)

    def gv_start(i, value):
        gvs[i] = value
        partner = me + (1 << i) - 2 * (1 << i) * lax.rem(me // (1 << i), 2)
        push(gvs.at[i], gvr.at[i], gv_s.at[i], gv_r.at[i], partner, view)

    def gv_next(i):
        arrived(gvr.at[i], gv_r.at[i])
        value = gvs[i] + gvr[i]
        if i + 1 < steps:
            gv_start(i + 1, value)
        else:
            vt_out[...] = vt_ref[...] - rate_view * value[:, :views]

    gv_start(0, SCALING * gv)

    order = [d % na for d in range(1, na + 1)]

    def turn(h, first, values):
        for t in range(texels):
            ysum[h, pl.ds(first + t, part, stride=2 * texels), :] = values[:, t * RL:(t + 1) * RL]

    for h in range(CHUNKS):
        total = ysend[h, view].astype(F32)
        for w in range(1, view_count):
            arrived(yrecv.at[h, w - 1], y_r.at[h, w - 1])
            total = total + yrecv[h, w - 1].astype(F32)
        ytot[h] = total.astype(BF)
        push(ytot.at[h], ysib.at[h], h_s.at[h], h_r.at[h], sibling, view)
        turn(h, 0, total)

    def u_rows(e):
        return jnp.concatenate(
            [uturn[slot(ahead(d), beside(e), core)] for d in order], axis=0).astype(BF)

    u_parts = [u_rows(e) for e in range(nb)]
    for h in range(CHUNKS):
        arrived(ysib.at[h], h_r.at[h])
        turn(h, texels, ysib[h].astype(F32))
        for j in range(0, part, 2):
            pair = jnp.concatenate(
                [ysum[h, 2 * texels * k:2 * texels * (k + 1), :] for k in (j, j + 1)], axis=1)
            yflat[h, :, j * RL:(j + 2) * RL] = pair.astype(BF)
        for e in range(1, nb):
            grad = SCALING * jnp.dot(u_parts[e], yflat[h], preferred_element_type=F32)
            for i, d in enumerate(order):
                xs[h, d, e - 1] = grad[i * rows:(i + 1) * rows].astype(BF)
                push(xs.at[h, d, e - 1], xr.at[h, d, e - 1], x_s.at[h, d, e - 1],
                     x_r.at[h, d, e - 1], slot(a, beside(e), core), view)
        grad = SCALING * jnp.dot(u_parts[0], yflat[h], preferred_element_type=F32)
        for i, d in enumerate(order):
            held[h, d] = grad[i * rows:(i + 1) * rows]
        if h == 0:
            gv_next(0)

    partial = jnp.zeros((2 * texels, RT // 2), F32)
    for h in range(CHUNKS):
        partial = partial + lax.dot_general(yflat[h], stacked(h), NT, preferred_element_type=F32)
    us[0] = SCALING * partial[:texels]
    us[1] = SCALING * partial[texels:]
    ubuf[view, core] = us[0]
    targets = [(1, sibling, view)]
    for w in range(1, view_count):
        targets += [(0, me, other(w)), (1, sibling, other(w))]
    for i, (half, tex, vw) in enumerate(targets):
        push(us.at[half], ubuf.at[view, core], u_s.at[i], u_r.at[view, core], tex, vw)

    own = []
    for h in range(CHUNKS):
        for d in order:
            block = held[h, d]
            for e in range(1, nb):
                arrived(xr.at[h, d, e - 1], x_r.at[h, d, e - 1])
                block = block + xr[h, d, e - 1].astype(F32)
            if d:
                zs[h, d - 1] = block.astype(BF)
                push(zs.at[h, d - 1], zr.at[h, d - 1], z_s.at[h, d - 1], z_r.at[h, d - 1],
                     slot(ahead(d), b, core), view)
        own.append(block)
        if h + 1 < steps:
            gv_next(h + 1)
    for i in range(CHUNKS + 1, steps):
        gv_next(i)
    arrived(ubuf.at[view, 1 - core], u_r.at[view, 1 - core])
    for w in range(1, view_count):
        for ci in range(2):
            arrived(ubuf.at[other(w), ci], u_r.at[other(w), ci])
    halves = [sum(ubuf[w, ci] for w in range(view_count)).T for ci in range(2)]
    total_u = jnp.concatenate(
        [halves[j % 2][j // 2 * rows:(j // 2 + 1) * rows] for j in range(tex_count)], axis=0).T
    u_out[...] = u_ref[...] - rate_tex * total_u
    for h in range(CHUNKS):
        block = own[h]
        for d in range(1, na):
            arrived(zr.at[h, d - 1], z_r.at[h, d - 1])
            block = block + zr[h, d - 1].astype(F32)
        block = rate_core * block
        for j in range(part):
            i = h * part + j
            at = pl.ds(i, rows, stride=band)
            core_out[at, :] = core_ref[at, :] - block[:, j * RL:(j + 1) * RL]
    for copy in pending:
        copy.wait_send()


def per_device(measured, view_mask, tex_factor, view_factor, light_factor, core_tensor):
    tex_count = lax.axis_size("tex")
    view_count = lax.axis_size("view")
    texels, views, _ = measured.shape
    rows, band, _ = core_tensor.shape
    part = band // CHUNKS
    cut = part * RL
    texels_all = texels * tex_count
    nb = tex_count // (2 * LINE)
    steps = tex_count.bit_length() - 1
    peers = max(view_count - 1, 1)
    across = max(nb - 1, 1)
    padded = 16 * (-(-views // 16))
    groups = texels // GROUP
    rates = (
        RT / (VALID * L),
        RV / (texels_all * L),
        RT * RV * RL / (texels_all * VALID * L),
    )
    vmem = pl.BlockSpec(memory_space=pltpu.VMEM)
    hbm = pl.BlockSpec(memory_space=pltpu.HBM)
    dma = pltpu.SemaphoreType.DMA
    tex_new, view_new, core_new = pl.pallas_call(
        functools.partial(kernel, tex_count, view_count, rates),
        out_shape=(
            jax.ShapeDtypeStruct((texels, RT), F32),
            jax.ShapeDtypeStruct((RV, views), F32),
            jax.ShapeDtypeStruct((rows * band, RL), F32),
        ),
        in_specs=[hbm] * 6,
        out_specs=(vmem, vmem, vmem),
        scratch_shapes=[
            pltpu.VMEM((rows * band, RL), F32),
            pltpu.VMEM((texels, RT), F32),
            pltpu.VMEM((RV, views), F32),
            pltpu.VMEM((1, views), jnp.int32),
            pltpu.VMEM((RL, L), BF),
            pltpu.VMEM((texels, RT), F32),
            pltpu.VMEM((tex_count, rows, 2 * texels), F32),
            pltpu.VMEM((2 * texels, RT // 2), BF),
            pltpu.VMEM((CHUNKS, rows, cut), BF),
            pltpu.VMEM((CHUNKS, LINE, nb, rows, cut), BF),
            pltpu.VMEM((L, texels, views), BF),
            pltpu.VMEM((L * texels, views), F32),
            pltpu.VMEM((texels, views, L), F32),
            pltpu.VMEM((views, LIGHTS), F32),
            pltpu.VMEM((padded, RV), F32),
            pltpu.VMEM((RV, padded), F32),
            pltpu.VMEM((GROUP * RL, GROUP * LIGHTS), BF),
            pltpu.VMEM((groups, padded, GROUP * RL), BF),
            pltpu.VMEM((groups, padded, GROUP * LIGHTS), BF),
            pltpu.VMEM((CHUNKS, texels, cut), F32),
            pltpu.VMEM((CHUNKS, texels, cut), F32),
            pltpu.VMEM((CHUNKS, part * texels, RL), F32),
            pltpu.VMEM((CHUNKS, view_count, part, texels * RL), BF),
            pltpu.VMEM((CHUNKS, view_count, part, texels * RL), BF),
            pltpu.VMEM((CHUNKS, peers, part, texels * RL), BF),
            pltpu.VMEM((CHUNKS, part * 2 * texels, RL), F32),
            pltpu.VMEM((CHUNKS, 2 * texels, cut), BF),
            pltpu.VMEM((CHUNKS, part, texels * RL), BF),
            pltpu.VMEM((CHUNKS, part, texels * RL), BF),
            pltpu.VMEM((2, texels, RT // 2), F32),
            pltpu.VMEM((view_count, 2, texels, RT // 2), F32),
            pltpu.VMEM((steps, RV, padded), F32),
            pltpu.VMEM((steps, RV, padded), F32),
            pltpu.VMEM((CHUNKS, LINE, across, rows, cut), BF),
            pltpu.VMEM((CHUNKS, LINE, across, rows, cut), BF),
            pltpu.VMEM((CHUNKS, LINE, rows, cut), F32),
            pltpu.VMEM((CHUNKS, LINE - 1, rows, cut), BF),
            pltpu.VMEM((CHUNKS, LINE - 1, rows, cut), BF),
            dma((6,)), dma, dma, dma((CHUNKS, LINE - 1)), dma((CHUNKS, LINE, across)),
            dma((CHUNKS, LINE, nb)), dma((CHUNKS,)), dma((CHUNKS,)),
            dma((CHUNKS, peers)), dma((CHUNKS, view_count)),
            dma((CHUNKS, peers)), dma((CHUNKS, peers)),
            dma((2 * peers + 1,)), dma((view_count, 2)), dma((steps,)), dma((steps,)),
            dma((CHUNKS,)), dma((CHUNKS,)),
            dma((CHUNKS, LINE, across)), dma((CHUNKS, LINE, across)),
            dma((CHUNKS, LINE - 1)), dma((CHUNKS, LINE - 1)),
        ],
        compiler_params=pltpu.CompilerParams(
            collective_id=0, has_side_effects=True, vmem_limit_bytes=48 * 1024 * 1024),
        cost_estimate=pl.CostEstimate(flops=10**9, bytes_accessed=10**7, transcendentals=0),
    )(*(pltpu.with_memory_space_constraint(x, pltpu.HBM) for x in (
        core_tensor.reshape(rows * band, RL), tex_factor, view_factor.T, view_mask.reshape(1, views), light_factor.T,
        jnp.transpose(measured, (2, 0, 1)))))
    return tex_new, view_new.T, core_new.reshape(core_tensor.shape)


def solution(mesh):
    return jax.shard_map(
        per_device,
        mesh=mesh,
        in_specs=(
            P("tex", "view", None),
            P("view"),
            P("tex", None),
            P("view", None),
            P(),
            P("tex", "view", None),
        ),
        out_specs=(P("tex", None), P("view", None), P("tex", "view", None)),
        check_vma=False,
    )
```

```python
import functools

import jax
import jax.numpy as jnp
from jax import lax
from jax.experimental import pallas as pl
from jax.experimental.pallas import tpu as pltpu
from jax.sharding import PartitionSpec as P

RT = 256
RV = 64
RL = 64
VALID = 151
L = 151
LINE = 4
CHUNKS = 2
GROUP = 256 // RL
LIGHTS = 256 * (-(-L // 256))
SCALING = (RT * RV * RL) ** (-0.5)
MESH = pl.DeviceIdType.MESH
BF = jnp.bfloat16
F32 = jnp.float32
NT = (((1,), (1,)), ((), ()))
TN = (((0,), (0,)), ((), ()))


def kernel(
    tex_count, view_count, rates,
    core_hbm, u_hbm, vt_hbm, mask_hbm, lightt_hbm, meas_hbm,
    u_out, vt_out, core_out,
    core_ref, u_ref, vt_ref, mask_ref, lightt_ref, usib, uturn, uown,
    gl, gbuf, meas, mwide, mturn, weights, vcol, vrow, bdw, qbuf, rbuf, psend, psib, p3, pall,
    ysend, yrecv, ysum, yflat, ytot, ysib, us, ubuf, gvs, gvr, xs, xr, held, zs, zr,
    in_sem, w_s, w_r, ga_s, gb_s, g_r, q_s, q_r, p_s, p_r, y_s, y_r, u_s, u_r, gv_s, gv_r,
    h_s, h_r, x_s, x_r, z_s, z_r,
):
    na = LINE
    nb = tex_count // (2 * na)
    me = lax.axis_index("tex")
    view = lax.axis_index("view")
    core = lax.rem(me, 2)
    b = lax.rem(me // 2, nb)
    a = me // (2 * nb)
    _, rows, cut = gl.shape
    part = cut // RL
    band = part * CHUNKS
    texels = u_ref.shape[0]
    views = vt_ref.shape[1]
    padded = vcol.shape[0]
    groups = texels // GROUP
    steps = tex_count.bit_length() - 1
    rate_tex, rate_view, rate_core = rates

    def slot(ai, bi, ci):
        return (ai * nb + bi) * 2 + ci

    def ahead(d):
        return lax.rem(a + d, na)

    def beside(e):
        return lax.rem(b + e, nb)

    def other(w):
        return lax.rem(view + w, view_count)

    sibling = slot(a, b, 1 - core)
    pending = []

    def push(src, dst, ssem, rsem, tex, vw):
        copy = pltpu.make_async_remote_copy(
            src_ref=src, dst_ref=dst, send_sem=ssem, recv_sem=rsem,
            device_id=(tex, vw), device_id_type=MESH,
        )
        copy.start()
        pending.append(copy)

    def arrived(ref, sem):
        pltpu.make_async_copy(ref, ref, sem).wait()

    barrier = pltpu.get_barrier_semaphore()
    peers = [(slot(ahead(d), b, core), view) for d in range(1, na)]
    peers += [(slot(a, beside(e), core), view) for e in range(1, nb)]
    peers += [(sibling, view)]
    peers += [(tex, other(w)) for w in range(1, view_count) for tex in (me, sibling)]
    for peer in peers:
        pl.semaphore_signal(barrier, inc=1, device_id=peer, device_id_type=MESH)
    fetches = [
        pltpu.make_async_copy(src, dst, in_sem.at[i]) for i, (src, dst) in enumerate((
            (core_hbm, core_ref), (u_hbm, u_ref), (meas_hbm, meas),
            (vt_hbm, vt_ref), (mask_hbm, mask_ref), (lightt_hbm, lightt_ref)))
    ]
    for fetch in fetches:
        fetch.start()
    fetches[0].wait()
    for i in range(0, band, 2):
        pair = jnp.concatenate(
            [core_ref[pl.ds(i + k, rows, stride=band), :] for k in range(2)], axis=1).astype(BF)
        h, o = divmod(i, part)
        gl[h, :, o * RL:(o + 2) * RL] = pair
    pl.semaphore_wait(barrier, len(peers))

    for h in range(CHUNKS):
        for e in range(1, nb):
            push(gl.at[h], gbuf.at[h, a, b], gb_s.at[h, 0, e - 1], g_r.at[h, a, b],
                 slot(a, beside(e), core), view)
        for d in range(1, na):
            push(gl.at[h], gbuf.at[h, a, b], ga_s.at[h, d - 1], g_r.at[h, a, b],
                 slot(ahead(d), b, core), view)
    fetches[1].wait()
    push(u_ref, usib, w_s, w_r, sibling, view)

    def from_line(h, d):
        ad = ahead(na - d)
        arrived(gbuf.at[h, ad, b], g_r.at[h, ad, b])
        for e in range(1, nb):
            push(gbuf.at[h, ad, b], gbuf.at[h, ad, b], gb_s.at[h, d, e - 1], g_r.at[h, ad, b],
                 slot(a, beside(e), core), view)

    def from_across(h):
        for d in range(na):
            for e in range(1, nb):
                ad, be = ahead(na - d), beside(nb - e)
                arrived(gbuf.at[h, ad, be], g_r.at[h, ad, be])

    for h in range(CHUNKS):
        gbuf[h, a, b] = gl[h]
    bdw[...] = jnp.zeros_like(bdw)
    rbuf[...] = jnp.zeros_like(rbuf)
    for fetch in fetches[2:]:
        fetch.wait()
    for j in range(GROUP):
        bdw[j * RL:(j + 1) * RL, j * LIGHTS:j * LIGHTS + L] = lightt_ref[...]
    vcol[...] = jnp.zeros_like(vcol)
    vrow[...] = jnp.zeros_like(vrow)
    vcol[:views, :] = vt_ref[...].T
    vrow[:, :views] = vt_ref[...]
    weights[...] = jnp.broadcast_to(mask_ref[...].astype(F32), (LIGHTS, views)).T
    mwide[...] = meas[...].astype(F32).reshape(mwide.shape)
    turns = texels // (2 * CHUNKS * (na - 1))
    t = 0
    for h in range(CHUNKS):
        for d in range(1, na):
            from_line(h, d)
            for _ in range(turns):
                mturn[t] = mwide[pl.ds(t, L, stride=texels), :].T
                t += 1
    while t < texels:
        mturn[t] = mwide[pl.ds(t, L, stride=texels), :].T
        t += 1

    arrived(usib, w_r)
    turned = jnp.concatenate([u_ref[...], usib[...]], axis=0).T
    for j in range(tex_count):
        uturn[j] = turned[j * rows:(j + 1) * rows]
    pairs = [(ai, bi) for ai in range(na) for bi in range(nb)]
    uown[...] = jnp.concatenate([uturn[slot(ai, bi, core)] for ai, bi in pairs], axis=0).T.astype(BF)
    u_own = uown[...]

    def stacked(h):
        if rows % 16 == 0:
            return gbuf[h].reshape(len(pairs) * rows, part * RL)
        return jnp.concatenate(
            [gbuf[h, ai, bi].astype(F32) for ai, bi in pairs], axis=0).astype(BF)

    kept = []

    def project(h):
        from_across(h)
        proj = jnp.dot(u_own, stacked(h), preferred_element_type=F32)
        psend[h] = proj[texels:]
        push(psend.at[h], psib.at[h], q_s.at[h], q_r.at[h], sibling, view)
        kept.append(proj[:texels])

    def exchange(h):
        arrived(psib.at[h], q_r.at[h])
        proj = kept[h] + psib[h]
        for j in range(part):
            p3[h, j * texels:(j + 1) * texels, :] = proj[:, j * RL:(j + 1) * RL]
        for t in range(0, texels, 2):
            pair = jnp.concatenate(
                [p3[h, pl.ds(t + k, part, stride=texels), :] for k in range(2)], axis=1)
            pall[h, view, :, t * RL:(t + 2) * RL] = pair.astype(BF)
        for w in range(1, view_count):
            push(pall.at[h, view], pall.at[h, view], p_s.at[h, w - 1], p_r.at[h, view],
                 me, other(w))

    project(0)
    for h in range(1, CHUNKS):
        exchange(h - 1)
        project(h)
    exchange(CHUNKS - 1)
    v_bf = vcol[...].astype(BF)
    vt_bf = vrow[...].astype(BF)
    for h in range(CHUNKS):
        for w in range(1, view_count):
            arrived(pall.at[h, other(w)], p_r.at[h, other(w)])

    def lanes(k):
        return slice(k * GROUP * RL, (k + 1) * GROUP * RL)

    def p_group(k):
        pieces = [pall[h, w, :, lanes(k)] for w in range(view_count) for h in range(CHUNKS)]
        if part % 16 == 0:
            return jnp.concatenate(pieces, axis=0)
        return jnp.concatenate([piece.astype(F32) for piece in pieces], axis=0).astype(BF)

    for k in range(groups):
        qbuf[k] = jnp.dot(v_bf, p_group(k), preferred_element_type=F32).astype(BF)
    q_all = qbuf[...].reshape(groups * padded, GROUP * RL)
    mask = weights[:, :L]
    for j in range(GROUP):
        cols = slice(j * LIGHTS, (j + 1) * LIGHTS)
        approx = jnp.dot(q_all, bdw[:, cols], preferred_element_type=F32)
        for k in range(groups):
            piece = approx[k * padded:k * padded + views, :L]
            resid = mask * (SCALING * piece - mturn[k * GROUP + j])
            rbuf[k, :views, j * LIGHTS:j * LIGHTS + L] = resid.astype(BF)
    r_all = rbuf[...].reshape(groups * padded, GROUP * LIGHTS)
    s_all = lax.dot_general(r_all, bdw[...], NT, preferred_element_type=F32).astype(BF)
    for k in range(groups):
        s4 = s_all[k * padded:(k + 1) * padded]
        y4 = jnp.dot(vt_bf, s4, preferred_element_type=F32).astype(BF)
        for w in range(view_count):
            for h in range(CHUNKS):
                first = w * band + h * part
                ysend[h, w, :, lanes(k)] = y4[first:first + part]
    for h in range(CHUNKS):
        for w in range(1, view_count):
            push(ysend.at[h, other(w)], yrecv.at[h, w - 1], y_s.at[h, w - 1], y_r.at[h, w - 1],
                 me, other(w))
    gv = jnp.zeros((RV, padded), F32)
    for k in range(groups):
        s4 = s_all[k * padded:(k + 1) * padded]
        gv = gv + lax.dot_general(p_group(k), s4, NT, preferred_element_type=F32)

    def gv_start(i, value):
        gvs[i] = value
        partner = me + (1 << i) - 2 * (1 << i) * lax.rem(me // (1 << i), 2)
        push(gvs.at[i], gvr.at[i], gv_s.at[i], gv_r.at[i], partner, view)

    def gv_next(i):
        arrived(gvr.at[i], gv_r.at[i])
        value = gvs[i] + gvr[i]
        if i + 1 < steps:
            gv_start(i + 1, value)
        else:
            vt_out[...] = vt_ref[...] - rate_view * value[:, :views]

    gv_start(0, SCALING * gv)

    order = [d % na for d in range(1, na + 1)]

    def turn(h, first, values):
        for t in range(texels):
            ysum[h, pl.ds(first + t, part, stride=2 * texels), :] = values[:, t * RL:(t + 1) * RL]

    def add_views(h):
        total = ysend[h, view].astype(F32)
        for w in range(1, view_count):
            arrived(yrecv.at[h, w - 1], y_r.at[h, w - 1])
            total = total + yrecv[h, w - 1].astype(F32)
        ytot[h] = total.astype(BF)
        push(ytot.at[h], ysib.at[h], h_s.at[h], h_r.at[h], sibling, view)
        turn(h, 0, total)

    def u_rows(e):
        return jnp.concatenate(
            [uturn[slot(ahead(d), beside(e), core)] for d in order], axis=0).astype(BF)

    u_parts = [u_rows(e) for e in range(nb)]
    add_views(0)
    for h in range(CHUNKS):
        arrived(ysib.at[h], h_r.at[h])
        turn(h, texels, ysib[h].astype(F32))
        for j in range(0, part, 2):
            pair = jnp.concatenate(
                [ysum[h, 2 * texels * k:2 * texels * (k + 1), :] for k in (j, j + 1)], axis=1)
            yflat[h, :, j * RL:(j + 2) * RL] = pair.astype(BF)
        for e in range(1, nb):
            grad = SCALING * jnp.dot(u_parts[e], yflat[h], preferred_element_type=F32)
            for i, d in enumerate(order):
                xs[h, d, e - 1] = grad[i * rows:(i + 1) * rows].astype(BF)
                push(xs.at[h, d, e - 1], xr.at[h, d, e - 1], x_s.at[h, d, e - 1],
                     x_r.at[h, d, e - 1], slot(a, beside(e), core), view)
        grad = SCALING * jnp.dot(u_parts[0], yflat[h], preferred_element_type=F32)
        for i, d in enumerate(order):
            held[h, d] = grad[i * rows:(i + 1) * rows]
        if h + 1 < CHUNKS:
            add_views(h + 1)
        if h == 0:
            gv_next(0)

    partial = jnp.zeros((2 * texels, RT // 2), F32)
    for h in range(CHUNKS):
        partial = partial + lax.dot_general(yflat[h], stacked(h), NT, preferred_element_type=F32)
    us[0] = SCALING * partial[:texels]
    us[1] = SCALING * partial[texels:]
    ubuf[view, core] = us[0]
    targets = [(1, sibling, view)]
    for w in range(1, view_count):
        targets += [(0, me, other(w)), (1, sibling, other(w))]
    for i, (half, tex, vw) in enumerate(targets):
        push(us.at[half], ubuf.at[view, core], u_s.at[i], u_r.at[view, core], tex, vw)

    own = []
    for h in range(CHUNKS):
        for d in order:
            block = held[h, d]
            for e in range(1, nb):
                arrived(xr.at[h, d, e - 1], x_r.at[h, d, e - 1])
                block = block + xr[h, d, e - 1].astype(F32)
            if d:
                zs[h, d - 1] = block.astype(BF)
                push(zs.at[h, d - 1], zr.at[h, d - 1], z_s.at[h, d - 1], z_r.at[h, d - 1],
                     slot(ahead(d), b, core), view)
        own.append(block)
        if h + 1 < steps:
            gv_next(h + 1)
    for i in range(CHUNKS + 1, steps):
        gv_next(i)
    arrived(ubuf.at[view, 1 - core], u_r.at[view, 1 - core])
    for w in range(1, view_count):
        for ci in range(2):
            arrived(ubuf.at[other(w), ci], u_r.at[other(w), ci])
    halves = [sum(ubuf[w, ci] for w in range(view_count)).T for ci in range(2)]
    total_u = jnp.concatenate(
        [halves[j % 2][j // 2 * rows:(j // 2 + 1) * rows] for j in range(tex_count)], axis=0).T
    u_out[...] = u_ref[...] - rate_tex * total_u
    for h in range(CHUNKS):
        block = own[h]
        for d in range(1, na):
            arrived(zr.at[h, d - 1], z_r.at[h, d - 1])
            block = block + zr[h, d - 1].astype(F32)
        block = rate_core * block
        for j in range(part):
            i = h * part + j
            at = pl.ds(i, rows, stride=band)
            core_out[at, :] = core_ref[at, :] - block[:, j * RL:(j + 1) * RL]
    for copy in pending:
        copy.wait_send()


def per_device(measured, view_mask, tex_factor, view_factor, light_factor, core_tensor):
    tex_count = lax.axis_size("tex")
    view_count = lax.axis_size("view")
    texels, views, _ = measured.shape
    rows, band, _ = core_tensor.shape
    part = band // CHUNKS
    cut = part * RL
    texels_all = texels * tex_count
    nb = tex_count // (2 * LINE)
    steps = tex_count.bit_length() - 1
    peers = max(view_count - 1, 1)
    across = max(nb - 1, 1)
    padded = 16 * (-(-views // 16))
    groups = texels // GROUP
    rates = (
        RT / (VALID * L),
        RV / (texels_all * L),
        RT * RV * RL / (texels_all * VALID * L),
    )
    vmem = pl.BlockSpec(memory_space=pltpu.VMEM)
    hbm = pl.BlockSpec(memory_space=pltpu.HBM)
    dma = pltpu.SemaphoreType.DMA
    tex_new, view_new, core_new = pl.pallas_call(
        functools.partial(kernel, tex_count, view_count, rates),
        out_shape=(
            jax.ShapeDtypeStruct((texels, RT), F32),
            jax.ShapeDtypeStruct((RV, views), F32),
            jax.ShapeDtypeStruct((rows * band, RL), F32),
        ),
        in_specs=[hbm] * 6,
        out_specs=(vmem, vmem, vmem),
        scratch_shapes=[
            pltpu.VMEM((rows * band, RL), F32),
            pltpu.VMEM((texels, RT), F32),
            pltpu.VMEM((RV, views), F32),
            pltpu.VMEM((1, views), jnp.int32),
            pltpu.VMEM((RL, L), BF),
            pltpu.VMEM((texels, RT), F32),
            pltpu.VMEM((tex_count, rows, 2 * texels), F32),
            pltpu.VMEM((2 * texels, RT // 2), BF),
            pltpu.VMEM((CHUNKS, rows, cut), BF),
            pltpu.VMEM((CHUNKS, LINE, nb, rows, cut), BF),
            pltpu.VMEM((L, texels, views), BF),
            pltpu.VMEM((L * texels, views), F32),
            pltpu.VMEM((texels, views, L), F32),
            pltpu.VMEM((views, LIGHTS), F32),
            pltpu.VMEM((padded, RV), F32),
            pltpu.VMEM((RV, padded), F32),
            pltpu.VMEM((GROUP * RL, GROUP * LIGHTS), BF),
            pltpu.VMEM((groups, padded, GROUP * RL), BF),
            pltpu.VMEM((groups, padded, GROUP * LIGHTS), BF),
            pltpu.VMEM((CHUNKS, texels, cut), F32),
            pltpu.VMEM((CHUNKS, texels, cut), F32),
            pltpu.VMEM((CHUNKS, part * texels, RL), F32),
            pltpu.VMEM((CHUNKS, view_count, part, texels * RL), BF),
            pltpu.VMEM((CHUNKS, view_count, part, texels * RL), BF),
            pltpu.VMEM((CHUNKS, peers, part, texels * RL), BF),
            pltpu.VMEM((CHUNKS, part * 2 * texels, RL), F32),
            pltpu.VMEM((CHUNKS, 2 * texels, cut), BF),
            pltpu.VMEM((CHUNKS, part, texels * RL), BF),
            pltpu.VMEM((CHUNKS, part, texels * RL), BF),
            pltpu.VMEM((2, texels, RT // 2), F32),
            pltpu.VMEM((view_count, 2, texels, RT // 2), F32),
            pltpu.VMEM((steps, RV, padded), F32),
            pltpu.VMEM((steps, RV, padded), F32),
            pltpu.VMEM((CHUNKS, LINE, across, rows, cut), BF),
            pltpu.VMEM((CHUNKS, LINE, across, rows, cut), BF),
            pltpu.VMEM((CHUNKS, LINE, rows, cut), F32),
            pltpu.VMEM((CHUNKS, LINE - 1, rows, cut), BF),
            pltpu.VMEM((CHUNKS, LINE - 1, rows, cut), BF),
            dma((6,)), dma, dma, dma((CHUNKS, LINE - 1)), dma((CHUNKS, LINE, across)),
            dma((CHUNKS, LINE, nb)), dma((CHUNKS,)), dma((CHUNKS,)),
            dma((CHUNKS, peers)), dma((CHUNKS, view_count)),
            dma((CHUNKS, peers)), dma((CHUNKS, peers)),
            dma((2 * peers + 1,)), dma((view_count, 2)), dma((steps,)), dma((steps,)),
            dma((CHUNKS,)), dma((CHUNKS,)),
            dma((CHUNKS, LINE, across)), dma((CHUNKS, LINE, across)),
            dma((CHUNKS, LINE - 1)), dma((CHUNKS, LINE - 1)),
        ],
        compiler_params=pltpu.CompilerParams(
            collective_id=0, has_side_effects=True, vmem_limit_bytes=48 * 1024 * 1024),
        cost_estimate=pl.CostEstimate(flops=10**9, bytes_accessed=10**7, transcendentals=0),
    )(*(pltpu.with_memory_space_constraint(x, pltpu.HBM) for x in (
        core_tensor.reshape(rows * band, RL), tex_factor, view_factor.T, view_mask.reshape(1, views), light_factor.T,
        jnp.transpose(measured, (2, 0, 1)))))
    return tex_new, view_new.T, core_new.reshape(core_tensor.shape)


def solution(mesh):
    return jax.shard_map(
        per_device,
        mesh=mesh,
        in_specs=(
            P("tex", "view", None),
            P("view"),
            P("tex", None),
            P("view", None),
            P(),
            P("tex", "view", None),
        ),
        out_specs=(P("tex", None), P("view", None), P("tex", "view", None)),
        check_vma=False,
    )
```

```python
import functools

import jax
import jax.numpy as jnp
from jax import lax
from jax.experimental import pallas as pl
from jax.experimental.pallas import tpu as pltpu
from jax.sharding import PartitionSpec as P

RT = 256
RV = 64
RL = 64
VALID = 151
L = 151
LINE = 4
CHUNKS = 2
GROUP = 256 // RL
LIGHTS = 256 * (-(-L // 256))
SCALING = (RT * RV * RL) ** (-0.5)
MESH = pl.DeviceIdType.MESH
BF = jnp.bfloat16
F32 = jnp.float32
NT = (((1,), (1,)), ((), ()))
TN = (((0,), (0,)), ((), ()))


def kernel(
    tex_count, view_count, rates,
    core_hbm, u_hbm, vt_hbm, mask_hbm, lightt_hbm, meas_hbm,
    u_out, vt_out, core_out,
    core_ref, u_ref, vt_ref, mask_ref, lightt_ref, usib, uturn, uown,
    gl, gbuf, meas, mwide, mturn, weights, vcol, vrow, bdw, qbuf, rbuf, psend, psib, p3, pall,
    ysend, yrecv, ysum, yflat, ytot, ysib, us, ubuf, gvs, gvr, xs, xr, held, zs, zr,
    in_sem, w_s, w_r, ga_s, gb_s, g_r, q_s, q_r, p_s, p_r, y_s, y_r, u_s, u_r, gv_s, gv_r,
    h_s, h_r, x_s, x_r, z_s, z_r,
):
    na = LINE
    nb = tex_count // (2 * na)
    me = lax.axis_index("tex")
    view = lax.axis_index("view")
    core = lax.rem(me, 2)
    b = lax.rem(me // 2, nb)
    a = me // (2 * nb)
    _, rows, cut = gl.shape
    part = cut // RL
    band = part * CHUNKS
    texels = u_ref.shape[0]
    views = vt_ref.shape[1]
    padded = vcol.shape[0]
    groups = texels // GROUP
    steps = tex_count.bit_length() - 1
    rate_tex, rate_view, rate_core = rates

    def slot(ai, bi, ci):
        return (ai * nb + bi) * 2 + ci

    def ahead(d):
        return lax.rem(a + d, na)

    def beside(e):
        return lax.rem(b + e, nb)

    def other(w):
        return lax.rem(view + w, view_count)

    sibling = slot(a, b, 1 - core)
    pending = []

    def push(src, dst, ssem, rsem, tex, vw):
        copy = pltpu.make_async_remote_copy(
            src_ref=src, dst_ref=dst, send_sem=ssem, recv_sem=rsem,
            device_id=(tex, vw), device_id_type=MESH,
        )
        copy.start()
        pending.append(copy)

    def arrived(ref, sem):
        pltpu.make_async_copy(ref, ref, sem).wait()

    barrier = pltpu.get_barrier_semaphore()
    peers = [(slot(ahead(d), b, core), view) for d in range(1, na)]
    peers += [(slot(a, beside(e), core), view) for e in range(1, nb)]
    peers += [(sibling, view)]
    peers += [(tex, other(w)) for w in range(1, view_count) for tex in (me, sibling)]
    for peer in peers:
        pl.semaphore_signal(barrier, inc=1, device_id=peer, device_id_type=MESH)
    fetches = [
        pltpu.make_async_copy(src, dst, in_sem.at[i]) for i, (src, dst) in enumerate((
            (core_hbm, core_ref), (u_hbm, u_ref), (meas_hbm, meas),
            (vt_hbm, vt_ref), (mask_hbm, mask_ref), (lightt_hbm, lightt_ref)))
    ]
    for fetch in fetches:
        fetch.start()
    fetches[0].wait()
    for i in range(0, band, 2):
        pair = jnp.concatenate(
            [core_ref[pl.ds(i + k, rows, stride=band), :] for k in range(2)], axis=1).astype(BF)
        h, o = divmod(i, part)
        gl[h, :, o * RL:(o + 2) * RL] = pair
    pl.semaphore_wait(barrier, len(peers))

    for h in range(CHUNKS):
        for e in range(1, nb):
            push(gl.at[h], gbuf.at[h, a, b], gb_s.at[h, 0, e - 1], g_r.at[h, a, b],
                 slot(a, beside(e), core), view)
        for d in range(1, na):
            push(gl.at[h], gbuf.at[h, a, b], ga_s.at[h, d - 1], g_r.at[h, a, b],
                 slot(ahead(d), b, core), view)
    fetches[1].wait()
    push(u_ref, usib, w_s, w_r, sibling, view)

    def from_line(h, d):
        ad = ahead(na - d)
        arrived(gbuf.at[h, ad, b], g_r.at[h, ad, b])
        for e in range(1, nb):
            push(gbuf.at[h, ad, b], gbuf.at[h, ad, b], gb_s.at[h, d, e - 1], g_r.at[h, ad, b],
                 slot(a, beside(e), core), view)

    def from_across(h):
        for d in range(na):
            for e in range(1, nb):
                ad, be = ahead(na - d), beside(nb - e)
                arrived(gbuf.at[h, ad, be], g_r.at[h, ad, be])

    for h in range(CHUNKS):
        gbuf[h, a, b] = gl[h]
    bdw[...] = jnp.zeros_like(bdw)
    rbuf[...] = jnp.zeros_like(rbuf)
    for fetch in fetches[2:]:
        fetch.wait()
    for j in range(GROUP):
        bdw[j * RL:(j + 1) * RL, j * LIGHTS:j * LIGHTS + L] = lightt_ref[...]
    vcol[...] = jnp.zeros_like(vcol)
    vrow[...] = jnp.zeros_like(vrow)
    vcol[:views, :] = vt_ref[...].T
    vrow[:, :views] = vt_ref[...]
    weights[...] = jnp.broadcast_to(mask_ref[...].astype(F32), (LIGHTS, views)).T
    mwide[...] = meas[...].astype(F32).reshape(mwide.shape)
    waiting = list(range(texels))

    def turn_measured(count):
        for _ in range(min(count, len(waiting))):
            t = waiting.pop(0)
            mturn[t] = mwide[pl.ds(t, L, stride=texels), :].T

    turns = texels // (2 * CHUNKS * (na - 1))
    for h in range(CHUNKS):
        for d in range(1, na):
            from_line(h, d)
            turn_measured(turns)

    arrived(usib, w_r)
    turned = jnp.concatenate([u_ref[...], usib[...]], axis=0).T
    for j in range(tex_count):
        uturn[j] = turned[j * rows:(j + 1) * rows]
    pairs = [(ai, bi) for ai in range(na) for bi in range(nb)]
    uown[...] = jnp.concatenate([uturn[slot(ai, bi, core)] for ai, bi in pairs], axis=0).T.astype(BF)
    u_own = uown[...]

    def stacked(h):
        if rows % 16 == 0:
            return gbuf[h].reshape(len(pairs) * rows, part * RL)
        return jnp.concatenate(
            [gbuf[h, ai, bi].astype(F32) for ai, bi in pairs], axis=0).astype(BF)

    kept = []

    def project(h):
        from_across(h)
        proj = jnp.dot(u_own, stacked(h), preferred_element_type=F32)
        psend[h] = proj[texels:]
        push(psend.at[h], psib.at[h], q_s.at[h], q_r.at[h], sibling, view)
        kept.append(proj[:texels])

    def exchange(h):
        arrived(psib.at[h], q_r.at[h])
        proj = kept[h] + psib[h]
        for j in range(part):
            p3[h, j * texels:(j + 1) * texels, :] = proj[:, j * RL:(j + 1) * RL]
        for t in range(0, texels, 2):
            pair = jnp.concatenate(
                [p3[h, pl.ds(t + k, part, stride=texels), :] for k in range(2)], axis=1)
            pall[h, view, :, t * RL:(t + 2) * RL] = pair.astype(BF)
        for w in range(1, view_count):
            push(pall.at[h, view], pall.at[h, view], p_s.at[h, w - 1], p_r.at[h, view],
                 me, other(w))

    project(0)
    for h in range(1, CHUNKS):
        turn_measured(turns * 2)
        exchange(h - 1)
        project(h)
    turn_measured(turns * 2)
    exchange(CHUNKS - 1)
    turn_measured(texels)
    v_bf = vcol[...].astype(BF)
    vt_bf = vrow[...].astype(BF)
    for h in range(CHUNKS):
        for w in range(1, view_count):
            arrived(pall.at[h, other(w)], p_r.at[h, other(w)])

    def lanes(k):
        return slice(k * GROUP * RL, (k + 1) * GROUP * RL)

    def p_group(k):
        pieces = [pall[h, w, :, lanes(k)] for w in range(view_count) for h in range(CHUNKS)]
        if part % 16 == 0:
            return jnp.concatenate(pieces, axis=0)
        return jnp.concatenate([piece.astype(F32) for piece in pieces], axis=0).astype(BF)

    for k in range(groups):
        qbuf[k] = jnp.dot(v_bf, p_group(k), preferred_element_type=F32).astype(BF)
    q_all = qbuf[...].reshape(groups * padded, GROUP * RL)
    mask = weights[:, :L]
    for j in range(GROUP):
        cols = slice(j * LIGHTS, (j + 1) * LIGHTS)
        approx = jnp.dot(q_all, bdw[:, cols], preferred_element_type=F32)
        for k in range(groups):
            piece = approx[k * padded:k * padded + views, :L]
            resid = mask * (SCALING * piece - mturn[k * GROUP + j])
            rbuf[k, :views, j * LIGHTS:j * LIGHTS + L] = resid.astype(BF)
    r_all = rbuf[...].reshape(groups * padded, GROUP * LIGHTS)
    s_all = lax.dot_general(r_all, bdw[...], NT, preferred_element_type=F32).astype(BF)
    for k in range(groups):
        s4 = s_all[k * padded:(k + 1) * padded]
        y4 = jnp.dot(vt_bf, s4, preferred_element_type=F32).astype(BF)
        for w in range(view_count):
            for h in range(CHUNKS):
                first = w * band + h * part
                ysend[h, w, :, lanes(k)] = y4[first:first + part]
    for h in range(CHUNKS):
        for w in range(1, view_count):
            push(ysend.at[h, other(w)], yrecv.at[h, w - 1], y_s.at[h, w - 1], y_r.at[h, w - 1],
                 me, other(w))
    gv = jnp.zeros((RV, padded), F32)
    for k in range(groups):
        s4 = s_all[k * padded:(k + 1) * padded]
        gv = gv + lax.dot_general(p_group(k), s4, NT, preferred_element_type=F32)

    def gv_start(i, value):
        gvs[i] = value
        partner = me + (1 << i) - 2 * (1 << i) * lax.rem(me // (1 << i), 2)
        push(gvs.at[i], gvr.at[i], gv_s.at[i], gv_r.at[i], partner, view)

    def gv_next(i):
        arrived(gvr.at[i], gv_r.at[i])
        value = gvs[i] + gvr[i]
        if i + 1 < steps:
            gv_start(i + 1, value)
        else:
            vt_out[...] = vt_ref[...] - rate_view * value[:, :views]

    gv_start(0, SCALING * gv)

    order = [d % na for d in range(1, na + 1)]

    def turn(h, first, values):
        for t in range(texels):
            ysum[h, pl.ds(first + t, part, stride=2 * texels), :] = values[:, t * RL:(t + 1) * RL]

    def add_views(h):
        total = ysend[h, view].astype(F32)
        for w in range(1, view_count):
            arrived(yrecv.at[h, w - 1], y_r.at[h, w - 1])
            total = total + yrecv[h, w - 1].astype(F32)
        ytot[h] = total.astype(BF)
        push(ytot.at[h], ysib.at[h], h_s.at[h], h_r.at[h], sibling, view)
        turn(h, 0, total)

    def u_rows(e):
        return jnp.concatenate(
            [uturn[slot(ahead(d), beside(e), core)] for d in order], axis=0).astype(BF)

    u_parts = [u_rows(e) for e in range(nb)]
    add_views(0)
    for h in range(CHUNKS):
        arrived(ysib.at[h], h_r.at[h])
        turn(h, texels, ysib[h].astype(F32))
        for j in range(0, part, 2):
            pair = jnp.concatenate(
                [ysum[h, 2 * texels * k:2 * texels * (k + 1), :] for k in (j, j + 1)], axis=1)
            yflat[h, :, j * RL:(j + 2) * RL] = pair.astype(BF)
        for e in range(1, nb):
            grad = SCALING * jnp.dot(u_parts[e], yflat[h], preferred_element_type=F32)
            for i, d in enumerate(order):
                xs[h, d, e - 1] = grad[i * rows:(i + 1) * rows].astype(BF)
                push(xs.at[h, d, e - 1], xr.at[h, d, e - 1], x_s.at[h, d, e - 1],
                     x_r.at[h, d, e - 1], slot(a, beside(e), core), view)
        grad = SCALING * jnp.dot(u_parts[0], yflat[h], preferred_element_type=F32)
        for i, d in enumerate(order):
            held[h, d] = grad[i * rows:(i + 1) * rows]
        if h + 1 < CHUNKS:
            add_views(h + 1)
        if h == 0:
            gv_next(0)

    partial = jnp.zeros((2 * texels, RT // 2), F32)
    for h in range(CHUNKS):
        partial = partial + lax.dot_general(yflat[h], stacked(h), NT, preferred_element_type=F32)
    us[0] = SCALING * partial[:texels]
    us[1] = SCALING * partial[texels:]
    ubuf[view, core] = us[0]
    targets = [(1, sibling, view)]
    for w in range(1, view_count):
        targets += [(0, me, other(w)), (1, sibling, other(w))]
    for i, (half, tex, vw) in enumerate(targets):
        push(us.at[half], ubuf.at[view, core], u_s.at[i], u_r.at[view, core], tex, vw)

    own = []
    for h in range(CHUNKS):
        for d in order:
            block = held[h, d]
            for e in range(1, nb):
                arrived(xr.at[h, d, e - 1], x_r.at[h, d, e - 1])
                block = block + xr[h, d, e - 1].astype(F32)
            if d:
                zs[h, d - 1] = block.astype(BF)
                push(zs.at[h, d - 1], zr.at[h, d - 1], z_s.at[h, d - 1], z_r.at[h, d - 1],
                     slot(ahead(d), b, core), view)
        own.append(block)
        if h + 1 < steps:
            gv_next(h + 1)
    for i in range(CHUNKS + 1, steps):
        gv_next(i)
    arrived(ubuf.at[view, 1 - core], u_r.at[view, 1 - core])
    for w in range(1, view_count):
        for ci in range(2):
            arrived(ubuf.at[other(w), ci], u_r.at[other(w), ci])
    halves = [sum(ubuf[w, ci] for w in range(view_count)).T for ci in range(2)]
    total_u = jnp.concatenate(
        [halves[j % 2][j // 2 * rows:(j // 2 + 1) * rows] for j in range(tex_count)], axis=0).T
    u_out[...] = u_ref[...] - rate_tex * total_u
    for h in range(CHUNKS):
        block = own[h]
        for d in range(1, na):
            arrived(zr.at[h, d - 1], z_r.at[h, d - 1])
            block = block + zr[h, d - 1].astype(F32)
        block = rate_core * block
        for j in range(part):
            i = h * part + j
            at = pl.ds(i, rows, stride=band)
            core_out[at, :] = core_ref[at, :] - block[:, j * RL:(j + 1) * RL]
    for copy in pending:
        copy.wait_send()


def per_device(measured, view_mask, tex_factor, view_factor, light_factor, core_tensor):
    tex_count = lax.axis_size("tex")
    view_count = lax.axis_size("view")
    texels, views, _ = measured.shape
    rows, band, _ = core_tensor.shape
    part = band // CHUNKS
    cut = part * RL
    texels_all = texels * tex_count
    nb = tex_count // (2 * LINE)
    steps = tex_count.bit_length() - 1
    peers = max(view_count - 1, 1)
    across = max(nb - 1, 1)
    padded = 16 * (-(-views // 16))
    groups = texels // GROUP
    rates = (
        RT / (VALID * L),
        RV / (texels_all * L),
        RT * RV * RL / (texels_all * VALID * L),
    )
    vmem = pl.BlockSpec(memory_space=pltpu.VMEM)
    hbm = pl.BlockSpec(memory_space=pltpu.HBM)
    dma = pltpu.SemaphoreType.DMA
    tex_new, view_new, core_new = pl.pallas_call(
        functools.partial(kernel, tex_count, view_count, rates),
        out_shape=(
            jax.ShapeDtypeStruct((texels, RT), F32),
            jax.ShapeDtypeStruct((RV, views), F32),
            jax.ShapeDtypeStruct((rows * band, RL), F32),
        ),
        in_specs=[hbm] * 6,
        out_specs=(vmem, vmem, vmem),
        scratch_shapes=[
            pltpu.VMEM((rows * band, RL), F32),
            pltpu.VMEM((texels, RT), F32),
            pltpu.VMEM((RV, views), F32),
            pltpu.VMEM((1, views), jnp.int32),
            pltpu.VMEM((RL, L), BF),
            pltpu.VMEM((texels, RT), F32),
            pltpu.VMEM((tex_count, rows, 2 * texels), F32),
            pltpu.VMEM((2 * texels, RT // 2), BF),
            pltpu.VMEM((CHUNKS, rows, cut), BF),
            pltpu.VMEM((CHUNKS, LINE, nb, rows, cut), BF),
            pltpu.VMEM((L, texels, views), BF),
            pltpu.VMEM((L * texels, views), F32),
            pltpu.VMEM((texels, views, L), F32),
            pltpu.VMEM((views, LIGHTS), F32),
            pltpu.VMEM((padded, RV), F32),
            pltpu.VMEM((RV, padded), F32),
            pltpu.VMEM((GROUP * RL, GROUP * LIGHTS), BF),
            pltpu.VMEM((groups, padded, GROUP * RL), BF),
            pltpu.VMEM((groups, padded, GROUP * LIGHTS), BF),
            pltpu.VMEM((CHUNKS, texels, cut), F32),
            pltpu.VMEM((CHUNKS, texels, cut), F32),
            pltpu.VMEM((CHUNKS, part * texels, RL), F32),
            pltpu.VMEM((CHUNKS, view_count, part, texels * RL), BF),
            pltpu.VMEM((CHUNKS, view_count, part, texels * RL), BF),
            pltpu.VMEM((CHUNKS, peers, part, texels * RL), BF),
            pltpu.VMEM((CHUNKS, part * 2 * texels, RL), F32),
            pltpu.VMEM((CHUNKS, 2 * texels, cut), BF),
            pltpu.VMEM((CHUNKS, part, texels * RL), BF),
            pltpu.VMEM((CHUNKS, part, texels * RL), BF),
            pltpu.VMEM((2, texels, RT // 2), F32),
            pltpu.VMEM((view_count, 2, texels, RT // 2), F32),
            pltpu.VMEM((steps, RV, padded), F32),
            pltpu.VMEM((steps, RV, padded), F32),
            pltpu.VMEM((CHUNKS, LINE, across, rows, cut), BF),
            pltpu.VMEM((CHUNKS, LINE, across, rows, cut), BF),
            pltpu.VMEM((CHUNKS, LINE, rows, cut), F32),
            pltpu.VMEM((CHUNKS, LINE - 1, rows, cut), BF),
            pltpu.VMEM((CHUNKS, LINE - 1, rows, cut), BF),
            dma((6,)), dma, dma, dma((CHUNKS, LINE - 1)), dma((CHUNKS, LINE, across)),
            dma((CHUNKS, LINE, nb)), dma((CHUNKS,)), dma((CHUNKS,)),
            dma((CHUNKS, peers)), dma((CHUNKS, view_count)),
            dma((CHUNKS, peers)), dma((CHUNKS, peers)),
            dma((2 * peers + 1,)), dma((view_count, 2)), dma((steps,)), dma((steps,)),
            dma((CHUNKS,)), dma((CHUNKS,)),
            dma((CHUNKS, LINE, across)), dma((CHUNKS, LINE, across)),
            dma((CHUNKS, LINE - 1)), dma((CHUNKS, LINE - 1)),
        ],
        compiler_params=pltpu.CompilerParams(
            collective_id=0, has_side_effects=True, vmem_limit_bytes=48 * 1024 * 1024),
        cost_estimate=pl.CostEstimate(flops=10**9, bytes_accessed=10**7, transcendentals=0),
    )(*(pltpu.with_memory_space_constraint(x, pltpu.HBM) for x in (
        core_tensor.reshape(rows * band, RL), tex_factor, view_factor.T, view_mask.reshape(1, views), light_factor.T,
        jnp.transpose(measured, (2, 0, 1)))))
    return tex_new, view_new.T, core_new.reshape(core_tensor.shape)


def solution(mesh):
    return jax.shard_map(
        per_device,
        mesh=mesh,
        in_specs=(
            P("tex", "view", None),
            P("view"),
            P("tex", None),
            P("view", None),
            P(),
            P("tex", "view", None),
        ),
        out_specs=(P("tex", None), P("view", None), P("tex", "view", None)),
        check_vma=False,
    )
```
